128 devices in a mesh: dp: 4 (over z), spatial: 16 (over y_hi, x, core), fsdp: 2 (over y_lo).
Axes of the slice: x: 4, y: 4 (y_hi: 2, y_lo: 2; y = y_hi * 2 + y_lo), z: 4, core: 2. Of those that a mesh axis runs over, the one named last changes fastest.
Arguments:
- features: bfloat16 [8, 128, 256, 256], P(('dp', 'fsdp'), 'spatial'), may hold values from -6 to 6
- geometry: int32 [8, 128, 256], P(('dp', 'fsdp'), 'spatial'), may hold values from 0 to 2
- bc_class: int32 [8], P(('dp', 'fsdp')), may hold values from 0 to 7, as said below
- code_scale: float32 [3, 256], replicated, may hold values from 0.5 to 2
- bc_bias: float32 [8, 256], replicated, may hold values from -3 to 3
- kernel_one: bfloat16 [3, 3, 256, 256], P(None, None, None, 'fsdp'), may hold values from -0.125 to 0.125
- kernel_two: bfloat16 [3, 3, 256, 256], P(None, None, None, 'fsdp'), may hold values from -0.125 to 0.125
- cotangent: bfloat16 [8, 128, 256, 256], P(('dp', 'fsdp'), 'spatial'), may hold values from -6 to 6
Outputs:
- grad_features: bfloat16 [8, 128, 256, 256], P(('dp', 'fsdp'), 'spatial')
- grad_one: float32 [3, 3, 256, 256], P(None, None, None, 'fsdp')
- grad_two: float32 [3, 3, 256, 256], P(None, None, None, 'fsdp')
The draws below stay inside these ranges and needn't reach their ends.
Inputs may be any that keep to these rules, and one draw needn't show every extreme that they name: `bc_class`: every class occurs among the samples.
All inputs are finite; a program needn't handle non-finite values.
Results may differ from the reference program's by a relative error of at most 0.0065.
Values may be sent and summed in bfloat16 or wider, within the bound.
A program may use at most 64 MiB of HBM per device.

```python
import math
import jax
import jax.numpy as jnp
from jax import lax

C = 256
NB = 8
WIDTH = 256
SAMPLES = 8
HEIGHT = 128


def draw_bc_class(key, part):
    order = jax.random.permutation(key, SAMPLES)
    return (order % NB).astype(jnp.int32)


def with_ends(result, stream_key, least, high):
    longest = result.shape.index(max(result.shape))
    spots = []
    for shift in (0, 1):
        where = [jax.random.randint(jax.random.fold_in(stream_key, axis), (), 0, length) for axis, length in enumerate(result.shape)]
        where[longest] = (where[longest] + shift) % result.shape[longest]
        spots.append(tuple(where))
    return result.at[spots[0]].set(least).at[spots[1]].set(high)


def shard_levels(key, dims, split, least, largest):
    def one(position, shards_of):
        heights = jax.random.uniform(jax.random.fold_in(jax.random.fold_in(key, 6), position), (shards_of,), jnp.float32, least / len(split), largest / len(split))
        return jnp.repeat(jnp.exp(heights), dims[position] // shards_of).reshape((-1,) + (1,) * (len(dims) - position - 1))

    loudness = one(*split[0])
    for cut in split[1:]:
        loudness = loudness * one(*cut)
    return loudness


def bell_draw(rng, dims, deviation, limit, pieces=(), dtype=jnp.bfloat16):
    array = deviation * jax.random.normal(rng, dims, jnp.float32)
    if pieces:
        array = array * shard_levels(rng, dims, pieces, -0.22, 0.18)
    return jnp.clip(array, -limit, limit).astype(dtype)


def setup_inputs(seed: int = 0) -> dict:
    key_list = jax.random.split(jax.random.key(seed), 9)
    features = bell_draw(key_list[0], (SAMPLES, HEIGHT, WIDTH, C), 1.0, 6.0, ((0, 8), (1, 16)))
    geometry = with_ends(jax.random.randint(key_list[1], (SAMPLES, HEIGHT, WIDTH), 0, 3), jax.random.fold_in(key_list[1], 1), 0, 2).astype(jnp.int32)
    bc_class = draw_bc_class(jax.random.fold_in(key_list[8], 71), 0)
    code_scale = jnp.clip(jnp.exp(jax.random.uniform(key_list[3], (3, C), jnp.float32, math.log(0.5), math.log(2.0))), 0.5, 2.0)
    bc_bias = bell_draw(key_list[4], (NB, C), 0.5, 3.0, (), jnp.float32)
    kernel_one = bell_draw(key_list[5], (3, 3, C, C), (9 * C) ** -0.5, 0.125, ((3, 2),))
    kernel_two = bell_draw(key_list[6], (3, 3, C, C), (9 * C) ** -0.5, 0.125, ((3, 2),))
    cotangent = bell_draw(key_list[7], (SAMPLES, HEIGHT, WIDTH, C), 1.0, 6.0, ((0, 8), (1, 16)))
    return {"features": features, "geometry": geometry, "bc_class": bc_class, "code_scale": code_scale, "bc_bias": bc_bias, "kernel_one": kernel_one, "kernel_two": kernel_two, "cotangent": cotangent}


def convolve(amap, kernel):
    return lax.conv_general_dilated(amap.astype(jnp.float32), kernel.astype(jnp.float32), (1, 1), ((1, 1), (1, 1)), dimension_numbers=('NHWC', 'HWIO', 'NHWC'))

def flipped(kernel):
    return jnp.transpose(kernel[::-1, ::-1], (0, 1, 3, 2))

def correlate(amap, grads):
    height = grads.shape[1]
    width = grads.shape[2]
    padded = jnp.pad(amap, ((0, 0), (1, 1), (1, 1), (0, 0)))
    gfloat = grads.astype(jnp.float32)
    rows_out = []
    for row_off in range(3):
        cols_out = []
        for col_off in range(3):
            window = padded[:, row_off:row_off + height, col_off:col_off + width, :].astype(jnp.float32)
            cols_out.append(jnp.einsum('nhwc,nhwo->co', window, gfloat))
        rows_out.append(jnp.stack(cols_out))
    return jnp.stack(rows_out)

def reference(features, geometry, bc_class, code_scale, bc_bias, kernel_one, kernel_two, cotangent):
    gain = code_scale[geometry]
    offset = bc_bias[bc_class][:, None, None, :]
    gated = (features.astype(jnp.float32) * gain + offset).astype(jnp.bfloat16)
    pre = convolve(gated, kernel_one)
    act = jax.nn.gelu(pre).astype(jnp.bfloat16)
    grad_act = convolve(cotangent, flipped(kernel_two))
    grad_pre = jax.vjp(jax.nn.gelu, pre)[1](grad_act)[0].astype(jnp.bfloat16)
    back = cotangent.astype(jnp.float32) + convolve(grad_pre, flipped(kernel_one))
    grad_features = (back * gain).astype(jnp.bfloat16)
    factor = 1.0 / math.sqrt(SAMPLES * HEIGHT * WIDTH)
    grad_two = correlate(act, cotangent) * factor
    grad_one = correlate(gated, grad_pre) * factor
    return (grad_features, grad_one, grad_two)
```

```python
import functools
import math

import jax
import jax.numpy as jnp
from jax import lax
from jax.experimental import pallas as pl
from jax.experimental.pallas import tpu as pltpu
from jax.sharding import PartitionSpec as P

MESH = pl.DeviceIdType.MESH
BF, F32 = jnp.bfloat16, jnp.float32
ROWS, WIDTH, C, HALF = 8, 256, 256, 128
CELLS = ROWS * WIDTH
QUARTER = 9 * C // 4
NN = (((1,), (0,)), ((), ()))
NT = (((1,), (1,)), ((), ()))
TN = (((0,), (0,)), ((), ()))
PIECES = 6
LINE_AXIS = ("z", "x", "z", "x", "z", "x")
SLOPE = math.sqrt(2.0 / math.pi)


def dot(a, b, dims):
    return lax.dot_general(a, b, dims, preferred_element_type=F32)


def put_shifted(value, low_ref, mid_ref, high_ref):
    place = lax.broadcasted_iota(jnp.int32, value.shape, 0)
    low_ref[...] = jnp.where(place == 0, 0.0, pltpu.roll(value, 1, 0)).astype(BF)
    mid_ref[...] = value.astype(BF)
    high_ref[...] = jnp.where(place == WIDTH - 1, 0.0, pltpu.roll(value, WIDTH - 1, 0)).astype(BF)


def body(
    feat, geo, bc, scale, bias, k1, k2, cot, gf, grads,
    fbuf, cbuf, gbuf, geot, sbuf, bbuf, gated_halo, cot_halo, pre_halo, edge,
    xg, xc, xp, w1, w2, pre, gact, act, part,
    sib_out, sib_in, plane_out, plane_in, line_out, line_in, shard,
    load_sem, halo_send, halo_recv, w_send, w_recv, r_send, r_recv,
):
    dp = lax.axis_index("dp")
    sp = lax.axis_index("spatial")
    fs = lax.axis_index("fsdp")
    core, cx, yh = sp % 2, (sp // 2) % 4, sp // 8
    cy = yh * 2 + fs
    other = 1 - fs

    def device(x, y, z, c):
        return (z, ((y // 2) * 4 + x) * 2 + c, y % 2)

    sibling = device(cx, cy, dp, 1 - core)
    up, down = (dp, sp - 1, fs), (dp, sp + 1, fs)
    has_up, has_down = sp > 0, sp < 15

    def peer(axis, k):
        side = k // 4
        y = (cy + k % 4) % 4
        if axis == "z":
            return (cx + side) % 4, y, dp
        return cx, y, (dp + side) % 4

    barrier = pltpu.get_barrier_semaphore()

    def greet(target):
        pl.semaphore_signal(barrier, inc=1, device_id=target, device_id_type=MESH)

    greet(sibling)
    pl.when(jnp.logical_and(core == 0, has_up))(lambda: greet(up))
    pl.when(jnp.logical_and(core == 1, has_down))(lambda: greet(down))

    def greet_z(k, _):
        greet(device(*peer("z", k), core))
        return 0

    def greet_x(k, _):
        greet(device(*peer("x", k), core))
        return 0

    lax.fori_loop(1, 16, greet_z, 0)
    lax.fori_loop(4, 16, greet_x, 0)

    def load(src, dst, i):
        cp = pltpu.make_async_copy(src, dst, load_sem.at[i])
        cp.start()
        return cp

    geo_cp = load(geo, gbuf, 0)
    scale_cp = load(scale, sbuf, 1)
    bias_cp = load(bias, bbuf, 2)
    feat_cp = load(feat, fbuf, 3)
    cot_cp = load(cot, cbuf, 4)
    k2_cp = load(k2, w2.at[fs], 5)
    k1_cp = load(k1, w1.at[fs], 6)

    strangers = jnp.where(core == 0, jnp.where(has_up, 1, 0), jnp.where(has_down, 1, 0))
    pl.semaphore_wait(barrier, 28 + strangers)

    def remote(src, dst, send, recv, target):
        return pltpu.make_async_remote_copy(
            src_ref=src, dst_ref=dst, send_sem=send, recv_sem=recv, device_id=target, device_id_type=MESH
        )

    def halo_up(src, n, buf):
        return remote(src, buf.at[1], halo_send.at[n, 0], halo_recv.at[n, 1], up)

    def halo_down(src, n, buf):
        return remote(src, buf.at[0], halo_send.at[n, 1], halo_recv.at[n, 0], down)

    top, bottom = pl.ds(0, WIDTH), pl.ds(CELLS - WIDTH, WIDTH)
    cot_up = halo_up(cot.at[top], 0, cot_halo)
    cot_down = halo_down(cot.at[bottom], 0, cot_halo)
    gated_up = halo_up(edge.at[0], 1, gated_halo)
    gated_down = halo_down(edge.at[1], 1, gated_halo)
    pre_up = halo_up(xp.at[pl.ds(WIDTH, WIDTH), pl.ds(C, C)], 2, pre_halo)
    pre_down = halo_down(xp.at[pl.ds(CELLS, WIDTH), pl.ds(C, C)], 2, pre_halo)
    pl.when(has_up)(lambda: cot_up.start())
    pl.when(has_down)(lambda: cot_down.start())

    next_a = device(cx, yh * 2 + other, dp, core)
    next_b = device(cx, (1 - yh) * 2 + other, dp, core)

    def quarter_copies(i, src, w):
        out = []
        for side, target in ((0, next_a), (1, next_b)):
            at = pl.ds(pl.multiple_of((2 * core + side) * QUARTER, 16), QUARTER)
            out.append(remote(src.at[at], w.at[fs, at], w_send.at[i, side], w_recv.at[i, side], target))
        at = pl.ds(pl.multiple_of(2 * core * QUARTER, 16), 2 * QUARTER)
        out.append(remote(w.at[other, at], w.at[other, at], w_send.at[i, 2], w_recv.at[i, 2], sibling))
        return out

    w1_copies = quarter_copies(0, k1, w1)
    w2_copies = quarter_copies(1, k2, w2)
    for cp in w1_copies[:2] + w2_copies[:2]:
        cp.start()

    geo_cp.wait()
    geot[...] = jnp.transpose(gbuf[...])
    scale_cp.wait()
    bias_cp.wait()
    classes = lax.broadcasted_iota(jnp.int32, (8, C), 0)
    offset = jnp.sum(jnp.where(classes == bc[0], bbuf[...], 0.0), axis=0, keepdims=True)

    def gain_of(row):
        code = geot[:, row : row + 1]
        return jnp.where(
            code == 0, sbuf[0:1, :], jnp.where(code == 1, sbuf[1:2, :], sbuf[2:3, :])
        )

    def put_row(x, r, value):
        at = pl.ds(r * WIDTH, WIDTH)
        put_shifted(value, x.at[at, pl.ds(0, C)], x.at[at, pl.ds(C, C)], x.at[at, pl.ds(2 * C, C)])

    def gated_row(row):
        f = fbuf[row * WIDTH : (row + 1) * WIDTH, :].astype(F32)
        return f * gain_of(row) + offset

    feat_cp.wait()
    first, last = gated_row(0), gated_row(ROWS - 1)
    edge[0] = first.astype(BF)
    edge[1] = last.astype(BF)
    pl.when(has_up)(lambda: gated_up.start())
    pl.when(has_down)(lambda: gated_down.start())
    for row in range(ROWS):
        put_row(xg, row + 1, gated_row(row))

    def put_cot(r, value):
        at = pl.ds(r * WIDTH, WIDTH)
        for h in range(2):
            put_shifted(
                value[:, h * HALF : (h + 1) * HALF],
                xc.at[h, at, pl.ds(0, HALF)],
                xc.at[h, at, pl.ds(HALF, HALF)],
                xc.at[h, at, pl.ds(2 * HALF, HALF)],
            )

    cot_cp.wait()
    for row in range(ROWS):
        put_cot(row + 1, cbuf[row * WIDTH : (row + 1) * WIDTH, :].astype(F32))

    def grad_act_half(h, r, rows):
        lhs = jnp.concatenate([xc[h, pl.ds((r + d) * WIDTH, rows * WIDTH), :] for d in range(3)], axis=1)
        rhs = jnp.concatenate([w2[h, (8 - t) * C : (9 - t) * C, :] for t in range(9)], axis=1)
        return dot(lhs, rhs, NT)

    k2_cp.wait()
    for r in (2, 4):
        gact[r * WIDTH : (r + 2) * WIDTH, :] = grad_act_half(fs, r, 2)

    def halo_rows(up_copy, down_copy, buf, put):
        @pl.when(has_up)
        def _():
            down_copy.wait_recv()
            put(0, buf[0].astype(F32))

        @pl.when(jnp.logical_not(has_up))
        def _():
            put(0, jnp.zeros((WIDTH, C), F32))

        @pl.when(has_down)
        def _():
            up_copy.wait_recv()
            put(ROWS + 1, buf[1].astype(F32))

        @pl.when(jnp.logical_not(has_down))
        def _():
            put(ROWS + 1, jnp.zeros((WIDTH, C), F32))

    halo_rows(cot_up, cot_down, cot_halo, put_cot)
    for r in (0, 6):
        gact[r * WIDTH : (r + 2) * WIDTH, :] = grad_act_half(fs, r, 2)
    for cp in w1_copies[:2]:
        cp.wait_recv()
    w1_copies[2].start()
    halo_rows(gated_up, gated_down, gated_halo, functools.partial(put_row, xg))
    k1_cp.wait()
    w1_copies[2].wait_recv()

    def big_lhs(x, r, rows):
        return jnp.concatenate([x[pl.ds((r + d) * WIDTH, rows * WIDTH), :] for d in range(3)], axis=1)

    pre[...] = dot(big_lhs(xg, 0, ROWS), jnp.concatenate([w1[0], w1[1]], axis=1), NN)
    for cp in w2_copies[:2]:
        cp.wait_recv()
    w2_copies[2].start()

    def act_row(row, _):
        at = pl.ds(pl.multiple_of(row * WIDTH, WIDTH), WIDTH)
        v = pre[at, :]
        act[at, :] = (0.5 * v * (1.0 + jnp.tanh(SLOPE * (v + 0.044715 * (v * v * v))))).astype(BF)
        return 0

    lax.fori_loop(0, ROWS, act_row, 0)

    def sib_copy(p):
        return remote(sib_out.at[p], sib_in.at[p], r_send.at[p, 0], r_recv.at[p, 0], sibling)

    def mine(p, source):
        return source[p, :, pl.ds(pl.multiple_of(core * HALF, HALF), HALF), :]

    def stage1(p):
        sib_out[p] = part[p, :, pl.ds(pl.multiple_of((1 - core) * HALF, HALF), HALF), :].astype(BF)
        sib_copy(p).start()

    def plane_wait(p):
        return remote(plane_in.at[p], plane_in.at[p], r_send.at[p, 1], r_recv.at[p, 1], sibling)

    def slot_of(x, y, z, axis):
        return (x if axis == "z" else z) * 4 + y

    def stage2(p):
        axis = LINE_AXIS[p]
        sib_copy(p).wait_recv()
        total = mine(p, part) + sib_in[p].astype(F32)
        for block in range(8):
            for h in range(2):
                plane_out[p, block * 2 + h] = total[
                    :, block * 16 : (block + 1) * 16, h * HALF : (h + 1) * HALF
                ].astype(BF)

        def send(k, _):
            to = peer(axis, k)
            remote(
                plane_out.at[p, slot_of(*to, axis)], plane_in.at[p, k - 1],
                r_send.at[p, 1], r_recv.at[p, 1], device(*to, core),
            ).start()
            return 0

        lax.fori_loop(1, 16, send, 0)

    def line_wait(p):
        return remote(line_in.at[p], line_in.at[p], r_send.at[p, 2], r_recv.at[p, 2], sibling)

    def stage3(p):
        axis = LINE_AXIS[p]
        plane_wait(p).wait_recv()
        total = plane_out[p, slot_of(cx, cy, dp, axis)].astype(F32)
        for k in range(15):
            total = total + plane_in[p, k].astype(F32)
        line_out[p] = total.astype(BF)

        def send(k, _):
            to = (cx, cy, (dp + k) % 4) if axis == "z" else ((cx + k) % 4, cy, dp)
            remote(
                line_out.at[p], line_in.at[p, k - 1], r_send.at[p, 2], r_recv.at[p, 2], device(*to, core)
            ).start()
            return 0

        lax.fori_loop(1, 4, send, 0)

    def row_of(block):
        return pl.ds(pl.multiple_of(core * HALF + block * 16, 16), 16)

    def gather_wait(p):
        few = plane_in.at[p, pl.ds(0, 7)]
        return remote(few, few, r_send.at[p, 3], r_recv.at[p, 3], sibling)

    def stage4(p):
        axis = LINE_AXIS[p]
        line_wait(p).wait_recv()
        total = line_out[p].astype(F32)
        for k in range(3):
            total = total + line_in[p, k].astype(F32)
        shard[p] = total.astype(BF)
        block = (cx if axis == "z" else dp) * 2 + yh
        grads[3 * p : 3 * p + 3, row_of(block), :] = total.astype(BF)

        def send(k, _):
            y = ((yh + k) % 2) * 2 + fs
            to = ((cx + k // 2) % 4, y, dp) if axis == "z" else (cx, y, (dp + k // 2) % 4)
            remote(
                shard.at[p], grads.at[pl.ds(3 * p, 3), row_of(block)],
                r_send.at[p, 3], r_recv.at[p, 3], device(*to, core),
            ).start()
            return 0

        lax.fori_loop(1, 8, send, 0)

    def last_copy(p):
        at = grads.at[pl.ds(3 * p, 3), pl.ds(pl.multiple_of(core * HALF, HALF), HALF)]
        return remote(at, at, r_send.at[p, 4], r_recv.at[p, 4], sibling)

    def stage5(p):
        gather_wait(p).wait_recv()
        last_copy(p).start()

    for d in range(3):
        for e in range(3):
            for h in range(2):
                part[d, e, :, h * HALF : (h + 1) * HALF] = dot(
                    act[...], xc[h, pl.ds((2 - d) * WIDTH, CELLS), (2 - e) * HALF : (3 - e) * HALF], TN
                )
        stage1(d)
        if d >= 1:
            stage2(d - 1)

    w2_copies[2].wait_recv()

    def grad_pre_rows(r):
        at = slice(r * WIDTH, (r + 2) * WIDTH)
        g = gact[at, :] + grad_act_half(other, r, 2)
        v = pre[at, :]
        sq = v * v
        t = jnp.tanh(SLOPE * (v + 0.044715 * (sq * v)))
        slope = 0.5 * (1.0 + t) + 0.5 * v * (1.0 - t * t) * (SLOPE * (1.0 + (3 * 0.044715) * sq))
        g = g * slope
        for i in range(2):
            put_row(xp, r + i + 1, g[i * WIDTH : (i + 1) * WIDTH])

    grad_pre_rows(0)
    pl.when(has_up)(lambda: pre_up.start())
    grad_pre_rows(6)
    pl.when(has_down)(lambda: pre_down.start())
    stage2(2)
    grad_pre_rows(2)
    stage3(0)
    grad_pre_rows(4)
    stage3(1)

    for d in range(3):
        p = 3 + d
        for e in range(3):
            part[p, e] = dot(
                xg[pl.ds(d * WIDTH, CELLS), e * C : (e + 1) * C], xp[pl.ds(WIDTH, CELLS), C : 2 * C], TN
            )
        stage1(p)
        if d == 0:
            stage3(2)
            stage4(0)
        elif d == 1:
            stage2(3)
            stage4(1)
        else:
            stage2(4)
            stage4(2)
            stage5(0)

    halo_rows(pre_up, pre_down, pre_halo, functools.partial(put_row, xp))

    def back_rows(r):
        rhs = jnp.concatenate(
            [jnp.concatenate([w1[0, (8 - t) * C : (9 - t) * C, :], w1[1, (8 - t) * C : (9 - t) * C, :]], axis=1) for t in range(9)],
            axis=1,
        )
        g = dot(big_lhs(xp, r, 2), rhs, NT)
        for i in range(2):
            at = slice((r + i) * WIDTH, (r + i + 1) * WIDTH)
            total = cbuf[at, :].astype(F32) + g[i * WIDTH : (i + 1) * WIDTH]
            fbuf[at, :] = (total * gain_of(r + i)).astype(BF)

    back_rows(0)
    stage2(5)
    stage3(3)
    back_rows(2)
    stage3(4)
    stage5(1)
    back_rows(4)
    stage3(5)
    stage4(3)
    back_rows(6)
    out_cp = pltpu.make_async_copy(fbuf, gf, load_sem.at[3])
    out_cp.start()
    stage4(4)
    stage5(2)
    stage4(5)
    stage5(3)
    stage5(4)
    stage5(5)
    for p in range(PIECES):
        last_copy(p).wait_recv()

    for p in range(PIECES):
        sib_copy(p).wait_send()
        plane_wait(p).wait_send()
        line_wait(p).wait_send()
        gather_wait(p).wait_send()
        last_copy(p).wait_send()
    for cp in w1_copies + w2_copies:
        cp.wait_send()
    for ups, downs in ((cot_up, cot_down), (gated_up, gated_down), (pre_up, pre_down)):
        pl.when(has_up)(lambda ups=ups: ups.wait_send())
        pl.when(has_down)(lambda downs=downs: downs.wait_send())
    out_cp.wait()


def on_device(features, geometry, bc_class, code_scale, bc_bias, kernel_one, kernel_two, cotangent):
    any_spec = pl.BlockSpec(memory_space=pl.ANY)
    vmem = pltpu.VMEM
    dma = pltpu.SemaphoreType.DMA
    grad_features, grads = pl.pallas_call(
        body,
        out_shape=(
            jax.ShapeDtypeStruct((CELLS, C), BF),
            jax.ShapeDtypeStruct((18, C, HALF), BF),
        ),
        in_specs=[any_spec, any_spec, pl.BlockSpec(memory_space=pltpu.SMEM)] + [any_spec] * 5,
        out_specs=(any_spec, pl.BlockSpec(memory_space=pltpu.VMEM)),
        scratch_shapes=[
            vmem((CELLS, C), BF),
            vmem((CELLS, C), BF),
            vmem((ROWS, WIDTH), jnp.int32),
            vmem((WIDTH, ROWS), jnp.int32),
            vmem((3, C), F32),
            vmem((8, C), F32),
            vmem((2, WIDTH, C), BF),
            vmem((2, WIDTH, C), BF),
            vmem((2, WIDTH, C), BF),
            vmem((2, WIDTH, C), BF),
            vmem((CELLS + 2 * WIDTH, 3 * C), BF),
            vmem((2, CELLS + 2 * WIDTH, 3 * HALF), BF),
            vmem((CELLS + 2 * WIDTH, 3 * C), BF),
            vmem((2, 9 * C, HALF), BF),
            vmem((2, 9 * C, HALF), BF),
            vmem((CELLS, C), F32),
            vmem((CELLS, C), F32),
            vmem((CELLS, C), BF),
            vmem((PIECES, 3, C, C), F32),
            vmem((PIECES, 3, HALF, C), BF),
            vmem((PIECES, 3, HALF, C), BF),
            vmem((PIECES, 16, 3, 16, HALF), BF),
            vmem((PIECES, 15, 3, 16, HALF), BF),
            vmem((PIECES, 3, 16, HALF), BF),
            vmem((PIECES, 3, 3, 16, HALF), BF),
            vmem((PIECES, 3, 16, HALF), BF),
            dma((7,)),
            dma((3, 2)),
            dma((3, 2)),
            dma((2, 3)),
            dma((2, 3)),
            dma((PIECES, 5)),
            dma((PIECES, 5)),
        ],
        compiler_params=pltpu.CompilerParams(
            collective_id=0, has_side_effects=True, vmem_limit_bytes=58 * 2**20
        ),
    )(
        features.reshape(CELLS, C),
        geometry.reshape(ROWS, WIDTH),
        bc_class,
        code_scale,
        bc_bias,
        kernel_one.reshape(9 * C, HALF),
        kernel_two.reshape(9 * C, HALF),
        cotangent.reshape(CELLS, C),
    )
    scaled = grads.astype(F32) * (1.0 / math.sqrt(8 * 128 * 256))
    scaled = scaled.reshape(2, 3, 3, C, HALF)
    return grad_features.reshape(features.shape), scaled[1], scaled[0]


def solution(mesh):
    placed = (
        P(("dp", "fsdp"), "spatial", None, None),
        P(("dp", "fsdp"), "spatial", None),
        P(("dp", "fsdp")),
        P(),
        P(),
        P(None, None, None, "fsdp"),
        P(None, None, None, "fsdp"),
        P(("dp", "fsdp"), "spatial", None, None),
    )
    return jax.shard_map(
        on_device,
        mesh=mesh,
        in_specs=placed,
        out_specs=(
            P(("dp", "fsdp"), "spatial", None, None),
            P(None, None, None, "fsdp"),
            P(None, None, None, "fsdp"),
        ),
        check_vma=False,
    )
```

```python
import functools
import math

import jax
import jax.numpy as jnp
from jax import lax
from jax.experimental import pallas as pl
from jax.experimental.pallas import tpu as pltpu
from jax.sharding import PartitionSpec as P

MESH = pl.DeviceIdType.MESH
BF, F32 = jnp.bfloat16, jnp.float32
ROWS, WIDTH, C, HALF = 8, 256, 256, 128
CELLS = ROWS * WIDTH
QUARTER = 9 * C // 4
NN = (((1,), (0,)), ((), ()))
NT = (((1,), (1,)), ((), ()))
TN = (((0,), (0,)), ((), ()))
PIECES = 6
LINE_AXIS = ("z", "y", "x", "z", "y", "x")
SLOPE = math.sqrt(2.0 / math.pi)


def dot(a, b, dims):
    return lax.dot_general(a, b, dims, preferred_element_type=F32)


def put_shifted(value, low_ref, mid_ref, high_ref):
    place = lax.broadcasted_iota(jnp.int32, value.shape, 0)
    low_ref[...] = jnp.where(place == 0, 0.0, pltpu.roll(value, 1, 0)).astype(BF)
    mid_ref[...] = value.astype(BF)
    high_ref[...] = jnp.where(place == WIDTH - 1, 0.0, pltpu.roll(value, WIDTH - 1, 0)).astype(BF)


def body(
    feat, geo, bc, scale, bias, k1, k2, cot, gf, g_two, g_one,
    fbuf, cbuf, gbuf, geot, sbuf, bbuf, gated_halo, cot_halo, pre_halo, edge,
    xg, xc, xp, w1, w2, pre, gact, act, part,
    sib_out, sib_in, plane_out, plane_in, line_out, line_in, shard,
    load_sem, hop_sem, halo_send, halo_recv, w_send, w_recv, r_send, r_recv,
):
    dp = lax.axis_index("dp")
    sp = lax.axis_index("spatial")
    fs = lax.axis_index("fsdp")
    core, cx, yh = sp % 2, (sp // 2) % 4, sp // 8
    cy = yh * 2 + fs
    other = 1 - fs

    def device(x, y, z, c):
        return (z, ((y // 2) * 4 + x) * 2 + c, y % 2)

    sibling = device(cx, cy, dp, 1 - core)
    up, down = (dp, sp - 1, fs), (dp, sp + 1, fs)
    has_up, has_down = sp > 0, sp < 15

    def peer(axis, k):
        side, step = k // 4, k % 4
        if axis == "z":
            return (cx + side) % 4, (cy + step) % 4, dp
        if axis == "y":
            return (cx + side) % 4, cy, (dp + step) % 4
        return cx, (cy + step) % 4, (dp + side) % 4

    barrier = pltpu.get_barrier_semaphore()

    def greet(target):
        pl.semaphore_signal(barrier, inc=1, device_id=target, device_id_type=MESH)

    ring = []
    for step in (1, 3):
        ring.append(device(cx, (cy + step) % 4, dp, core))
        ring.append(device((cx + step) % 4, cy, dp, core))
        ring.append(device(cx, cy, (dp + step) % 4, core))
    greet(sibling)
    for target in ring:
        greet(target)
    pl.when(jnp.logical_and(core == 0, has_up))(lambda: greet(up))
    pl.when(jnp.logical_and(core == 1, has_down))(lambda: greet(down))

    def tell(n):
        for target in ring:
            pl.semaphore_signal(hop_sem.at[n], inc=1, device_id=target, device_id_type=MESH)

    def heard(n):
        pl.semaphore_wait(hop_sem.at[n], 6)

    def load(src, dst, i):
        cp = pltpu.make_async_copy(src, dst, load_sem.at[i])
        cp.start()
        return cp

    geo_cp = load(geo, gbuf, 0)
    scale_cp = load(scale, sbuf, 1)
    bias_cp = load(bias, bbuf, 2)
    feat_cp = load(feat, fbuf, 3)
    cot_cp = load(cot, cbuf, 4)
    k2_cp = load(k2, w2.at[fs], 5)
    k1_cp = load(k1, w1.at[fs], 6)

    def remote(src, dst, send, recv, target):
        return pltpu.make_async_remote_copy(
            src_ref=src, dst_ref=dst, send_sem=send, recv_sem=recv, device_id=target, device_id_type=MESH
        )

    def halo_up(src, n, buf):
        return remote(src, buf.at[1], halo_send.at[n, 0], halo_recv.at[n, 1], up)

    def halo_down(src, n, buf):
        return remote(src, buf.at[0], halo_send.at[n, 1], halo_recv.at[n, 0], down)

    top, bottom = pl.ds(0, WIDTH), pl.ds(CELLS - WIDTH, WIDTH)
    cot_up = halo_up(cot.at[top], 0, cot_halo)
    cot_down = halo_down(cot.at[bottom], 0, cot_halo)
    gated_up = halo_up(edge.at[0], 1, gated_halo)
    gated_down = halo_down(edge.at[1], 1, gated_halo)
    pre_up = halo_up(xp.at[pl.ds(WIDTH, WIDTH), pl.ds(C, C)], 2, pre_halo)
    pre_down = halo_down(xp.at[pl.ds(CELLS, WIDTH), pl.ds(C, C)], 2, pre_halo)

    next_a = device(cx, yh * 2 + other, dp, core)
    next_b = device(cx, (1 - yh) * 2 + other, dp, core)

    def quarter_copies(i, src, w):
        out = []
        for side, target in ((0, next_a), (1, next_b)):
            at = pl.ds(pl.multiple_of((2 * core + side) * QUARTER, 16), QUARTER)
            out.append(remote(src.at[at], w.at[fs, at], w_send.at[i, side], w_recv.at[i, side], target))
        at = pl.ds(pl.multiple_of(2 * core * QUARTER, 16), 2 * QUARTER)
        out.append(remote(w.at[other, at], w.at[other, at], w_send.at[i, 2], w_recv.at[i, 2], sibling))
        return out

    w1_copies = quarter_copies(0, k1, w1)
    w2_copies = quarter_copies(1, k2, w2)

    geo_cp.wait()
    geot[...] = jnp.transpose(gbuf[...])
    scale_cp.wait()
    bias_cp.wait()
    classes = lax.broadcasted_iota(jnp.int32, (8, C), 0)
    offset = jnp.sum(jnp.where(classes == bc[0], bbuf[...], 0.0), axis=0, keepdims=True)

    def gain_of(row):
        code = geot[:, row : row + 1]
        return jnp.where(
            code == 0, sbuf[0:1, :], jnp.where(code == 1, sbuf[1:2, :], sbuf[2:3, :])
        )

    def put_row(x, r, value):
        at = pl.ds(r * WIDTH, WIDTH)
        put_shifted(value, x.at[at, pl.ds(0, C)], x.at[at, pl.ds(C, C)], x.at[at, pl.ds(2 * C, C)])

    def gated_row(row):
        f = fbuf[row * WIDTH : (row + 1) * WIDTH, :].astype(F32)
        return f * gain_of(row) + offset

    feat_cp.wait()
    for row in (0, 7, 1, 2, 3, 4, 5, 6):
        value = gated_row(row)
        put_row(xg, row + 1, value)
        if row in (0, 7):
            edge[row // 7] = value.astype(BF)

    strangers = jnp.where(core == 0, jnp.where(has_up, 1, 0), jnp.where(has_down, 1, 0))
    pl.semaphore_wait(barrier, 7 + strangers)
    for cp in w1_copies[:2]:
        cp.start()
    pl.when(has_up)(lambda: cot_up.start())
    pl.when(has_down)(lambda: cot_down.start())
    pl.when(has_up)(lambda: gated_up.start())
    pl.when(has_down)(lambda: gated_down.start())
    for cp in w2_copies[:2]:
        cp.start()
    tell(0)

    def put_cot(r, value):
        at = pl.ds(r * WIDTH, WIDTH)
        for h in range(2):
            put_shifted(
                value[:, h * HALF : (h + 1) * HALF],
                xc.at[h, at, pl.ds(0, HALF)],
                xc.at[h, at, pl.ds(HALF, HALF)],
                xc.at[h, at, pl.ds(2 * HALF, HALF)],
            )

    cot_cp.wait()
    for row in range(ROWS):
        put_cot(row + 1, cbuf[row * WIDTH : (row + 1) * WIDTH, :].astype(F32))

    def grad_act_half(h, r, rows):
        lhs = jnp.concatenate([xc[h, pl.ds((r + d) * WIDTH, rows * WIDTH), :] for d in range(3)], axis=1)
        rhs = jnp.concatenate([w2[h, (8 - t) * C : (9 - t) * C, :] for t in range(9)], axis=1)
        return dot(lhs, rhs, NT)

    k2_cp.wait()
    for r in (2, 4):
        gact[r * WIDTH : (r + 2) * WIDTH, :] = grad_act_half(fs, r, 2)

    def halo_rows(up_copy, down_copy, buf, put):
        @pl.when(has_up)
        def _():
            down_copy.wait_recv()
            put(0, buf[0].astype(F32))

        @pl.when(jnp.logical_not(has_up))
        def _():
            put(0, jnp.zeros((WIDTH, C), F32))

        @pl.when(has_down)
        def _():
            up_copy.wait_recv()
            put(ROWS + 1, buf[1].astype(F32))

        @pl.when(jnp.logical_not(has_down))
        def _():
            put(ROWS + 1, jnp.zeros((WIDTH, C), F32))

    heard(0)
    tell(1)
    halo_rows(cot_up, cot_down, cot_halo, put_cot)
    for r in (0, 6):
        gact[r * WIDTH : (r + 2) * WIDTH, :] = grad_act_half(fs, r, 2)
    for cp in w1_copies[:2]:
        cp.wait_recv()
    w1_copies[2].start()
    halo_rows(gated_up, gated_down, gated_halo, functools.partial(put_row, xg))
    k1_cp.wait()
    w1_copies[2].wait_recv()

    heard(1)
    tell(2)

    def big_lhs(x, r, rows):
        return jnp.concatenate([x[pl.ds((r + d) * WIDTH, rows * WIDTH), :] for d in range(3)], axis=1)

    pre[...] = dot(big_lhs(xg, 0, ROWS), jnp.concatenate([w1[0], w1[1]], axis=1), NN)
    for cp in w2_copies[:2]:
        cp.wait_recv()
    w2_copies[2].start()

    def act_row(row, _):
        at = pl.ds(pl.multiple_of(row * WIDTH, WIDTH), WIDTH)
        v = pre[at, :]
        act[at, :] = (0.5 * v * (1.0 + jnp.tanh(SLOPE * (v + 0.044715 * (v * v * v))))).astype(BF)
        return 0

    lax.fori_loop(0, ROWS, act_row, 0)
    heard(2)

    def sib_copy(p):
        return remote(sib_out.at[p], sib_in.at[p], r_send.at[p, 0], r_recv.at[p, 0], sibling)

    def mine(p, source):
        return source[p, :, pl.ds(pl.multiple_of(core * HALF, HALF), HALF), :]

    def stage1(p):
        sib_out[p] = part[p, :, pl.ds(pl.multiple_of((1 - core) * HALF, HALF), HALF), :].astype(BF)
        sib_copy(p).start()

    def plane_wait(p):
        return remote(plane_in.at[p], plane_in.at[p], r_send.at[p, 1], r_recv.at[p, 1], sibling)

    def slot_of(x, y, z, axis):
        return {"z": x * 4 + y, "y": x * 4 + z, "x": z * 4 + y}[axis]

    keeps = dp % 2 == fs

    def stage2(p):
        axis = LINE_AXIS[p]
        sib_copy(p).wait_recv()
        total = mine(p, part) + sib_in[p].astype(F32)
        for block in range(8):
            for h in range(2):
                plane_out[p, block * 2 + h] = total[
                    :, block * 16 : (block + 1) * 16, h * HALF : (h + 1) * HALF
                ].astype(BF)

        def send(k, _):
            to = peer(axis, k)
            remote(
                plane_out.at[p, slot_of(*to, axis)], plane_in.at[p, k - 1],
                r_send.at[p, 1], r_recv.at[p, 1], device(*to, core),
            ).start()
            return 0

        lax.fori_loop(1, 16, send, 0)

    def line_wait(p):
        return remote(line_in.at[p], line_in.at[p], r_send.at[p, 2], r_recv.at[p, 2], sibling)

    def stage3(p):
        axis = LINE_AXIS[p]
        plane_wait(p).wait_recv()
        total = plane_out[p, slot_of(cx, cy, dp, axis)].astype(F32)
        for k in range(15):
            total = total + plane_in[p, k].astype(F32)
        line_out[p] = total.astype(BF)

        def send(k, _):
            to = {
                "z": (cx, cy, (dp + k) % 4), "y": (cx, (cy + k) % 4, dp), "x": ((cx + k) % 4, cy, dp)
            }[axis]

            def go():
                remote(
                    line_out.at[p], line_in.at[p, k - 1], r_send.at[p, 2], r_recv.at[p, 2], device(*to, core)
                ).start()

            if axis == "y":
                pl.when((cy + k) % 2 == dp % 2)(go)
            else:
                go()
            return 0

        lax.fori_loop(1, 4, send, 0)

    def row_of(block):
        return pl.ds(pl.multiple_of(core * HALF + block * 16, 16), 16)

    def line_send_wait(p):
        def some(n):
            return remote(line_in.at[p, pl.ds(0, n)], line_in.at[p, pl.ds(0, n)], r_send.at[p, 2], r_recv.at[p, 2], sibling)

        if LINE_AXIS[p] == "y":
            pl.when(keeps)(lambda: some(1).wait_send())
            pl.when(jnp.logical_not(keeps))(lambda: some(2).wait_send())
        else:
            some(3).wait_send()

    def gather_wait(p, n):
        some = plane_in.at[p, pl.ds(0, n)]
        return remote(some, some, r_send.at[p, 3], r_recv.at[p, 3], sibling)

    def gather_recv_wait(p):
        if LINE_AXIS[p] == "y":
            pl.when(keeps)(lambda: gather_wait(p, 7).wait_recv())
            pl.when(jnp.logical_not(keeps))(lambda: gather_wait(p, 8).wait_recv())
        else:
            gather_wait(p, 7).wait_recv()

    def gather_send_wait(p):
        if LINE_AXIS[p] == "y":
            pl.when(keeps)(lambda: gather_wait(p, 15).wait_send())
        else:
            gather_wait(p, 7).wait_send()

    def finish_shard(p):
        axis = LINE_AXIS[p]
        line_wait(p).wait_recv()
        total = line_out[p].astype(F32)
        for k in range(3):
            total = total + line_in[p, k].astype(F32)
        shard[p] = total.astype(BF)
        block = {"z": cx * 2 + yh, "y": cx * 2 + dp // 2, "x": dp * 2 + yh}[axis]
        three = pl.ds(3 * (p % 3), 3)
        grads = (g_two, g_one)[p // 3]
        grads[three, row_of(block), :] = total.astype(BF)

        def send(k, _):
            y = ((yh + k) % 2) * 2 + fs
            if axis == "z":
                to = (cx + k // 2) % 4, y, dp
            elif axis == "y":
                to = peer("y", k)
            else:
                to = cx, y, (dp + k // 2) % 4
            remote(
                shard.at[p], grads.at[three, row_of(block)],
                r_send.at[p, 3], r_recv.at[p, 3], device(*to, core),
            ).start()
            return 0

        lax.fori_loop(1, 16 if axis == "y" else 8, send, 0)

    def stage4(p):
        if LINE_AXIS[p] == "y":
            pl.when(keeps)(lambda: finish_shard(p))
        else:
            finish_shard(p)

    def last_copy(p):
        at = (g_two, g_one)[p // 3].at[pl.ds(3 * (p % 3), 3), pl.ds(pl.multiple_of(core * HALF, HALF), HALF)]
        return remote(at, at, r_send.at[p, 4], r_recv.at[p, 4], sibling)

    def stage5(p):
        gather_recv_wait(p)
        last_copy(p).start()

    for d in range(3):
        for e in range(3):
            at, lanes = pl.ds((2 - d) * WIDTH, CELLS), slice((2 - e) * HALF, (3 - e) * HALF)
            part[d, e] = dot(act[...], jnp.concatenate([xc[0, at, lanes], xc[1, at, lanes]], axis=1), TN)
        stage1(d)
        if d >= 1:
            stage2(d - 1)

    w2_copies[2].wait_recv()

    def grad_pre_rows(r):
        at = slice(r * WIDTH, (r + 2) * WIDTH)
        g = gact[at, :] + grad_act_half(other, r, 2)
        v = pre[at, :]
        sq = v * v
        t = jnp.tanh(SLOPE * (v + 0.044715 * (sq * v)))
        slope = 0.5 * (1.0 + t) + 0.5 * v * (1.0 - t * t) * (SLOPE * (1.0 + (3 * 0.044715) * sq))
        g = g * slope
        for i in range(2):
            put_row(xp, r + i + 1, g[i * WIDTH : (i + 1) * WIDTH])

    grad_pre_rows(0)
    pl.when(has_up)(lambda: pre_up.start())
    grad_pre_rows(6)
    pl.when(has_down)(lambda: pre_down.start())
    stage2(2)
    grad_pre_rows(2)
    stage3(0)
    grad_pre_rows(4)
    stage3(1)

    for d in range(3):
        p = 3 + d
        for e in range(3):
            part[p, e] = dot(
                xg[pl.ds(d * WIDTH, CELLS), e * C : (e + 1) * C], xp[pl.ds(WIDTH, CELLS), C : 2 * C], TN
            )
        stage1(p)
        if d == 0:
            stage3(2)
            stage4(0)
        elif d == 1:
            stage2(3)
            stage4(1)
        else:
            stage2(4)
            stage4(2)
            stage5(0)

    halo_rows(pre_up, pre_down, pre_halo, functools.partial(put_row, xp))

    def back_rows(r):
        rhs = jnp.concatenate(
            [jnp.concatenate([w1[0, (8 - t) * C : (9 - t) * C, :], w1[1, (8 - t) * C : (9 - t) * C, :]], axis=1) for t in range(9)],
            axis=1,
        )
        g = dot(big_lhs(xp, r, 2), rhs, NT)
        for i in range(2):
            at = slice((r + i) * WIDTH, (r + i + 1) * WIDTH)
            total = cbuf[at, :].astype(F32) + g[i * WIDTH : (i + 1) * WIDTH]
            fbuf[at, :] = (total * gain_of(r + i)).astype(BF)

    back_rows(0)
    stage2(5)
    stage3(3)
    back_rows(2)
    stage3(4)
    stage5(1)
    back_rows(4)
    stage3(5)
    stage4(3)
    back_rows(6)
    out_cp = pltpu.make_async_copy(fbuf, gf, load_sem.at[3])
    out_cp.start()
    stage4(4)
    stage5(2)
    stage4(5)
    stage5(3)
    stage5(4)
    stage5(5)
    for p in range(PIECES):
        last_copy(p).wait_recv()

    for p in range(PIECES):
        sib_copy(p).wait_send()
        plane_wait(p).wait_send()
        line_send_wait(p)
        gather_send_wait(p)
        last_copy(p).wait_send()
    for cp in w1_copies + w2_copies:
        cp.wait_send()
    for ups, downs in ((cot_up, cot_down), (gated_up, gated_down), (pre_up, pre_down)):
        pl.when(has_up)(lambda ups=ups: ups.wait_send())
        pl.when(has_down)(lambda downs=downs: downs.wait_send())
    out_cp.wait()


def on_device(features, geometry, bc_class, code_scale, bc_bias, kernel_one, kernel_two, cotangent):
    any_spec = pl.BlockSpec(memory_space=pl.ANY)
    vmem = pltpu.VMEM
    dma = pltpu.SemaphoreType.DMA
    grad_features, g_two, g_one = pl.pallas_call(
        body,
        out_shape=(
            jax.ShapeDtypeStruct((CELLS, C), BF),
            jax.ShapeDtypeStruct((9, C, HALF), BF),
            jax.ShapeDtypeStruct((9, C, HALF), BF),
        ),
        in_specs=[any_spec, any_spec, pl.BlockSpec(memory_space=pltpu.SMEM)] + [any_spec] * 5,
        out_specs=(any_spec, pl.BlockSpec(memory_space=pltpu.VMEM), pl.BlockSpec(memory_space=pltpu.VMEM)),
        scratch_shapes=[
            vmem((CELLS, C), BF),
            vmem((CELLS, C), BF),
            vmem((ROWS, WIDTH), jnp.int32),
            vmem((WIDTH, ROWS), jnp.int32),
            vmem((3, C), F32),
            vmem((8, C), F32),
            vmem((2, WIDTH, C), BF),
            vmem((2, WIDTH, C), BF),
            vmem((2, WIDTH, C), BF),
            vmem((2, WIDTH, C), BF),
            vmem((CELLS + 2 * WIDTH, 3 * C), BF),
            vmem((2, CELLS + 2 * WIDTH, 3 * HALF), BF),
            vmem((CELLS + 2 * WIDTH, 3 * C), BF),
            vmem((2, 9 * C, HALF), BF),
            vmem((2, 9 * C, HALF), BF),
            vmem((CELLS, C), F32),
            vmem((CELLS, C), F32),
            vmem((CELLS, C), BF),
            vmem((PIECES, 3, C, C), F32),
            vmem((PIECES, 3, HALF, C), BF),
            vmem((PIECES, 3, HALF, C), BF),
            vmem((PIECES, 16, 3, 16, HALF), BF),
            vmem((PIECES, 15, 3, 16, HALF), BF),
            vmem((PIECES, 3, 16, HALF), BF),
            vmem((PIECES, 3, 3, 16, HALF), BF),
            vmem((PIECES, 3, 16, HALF), BF),
            dma((7,)),
            pltpu.SemaphoreType.REGULAR((3,)),
            dma((3, 2)),
            dma((3, 2)),
            dma((2, 3)),
            dma((2, 3)),
            dma((PIECES, 5)),
            dma((PIECES, 5)),
        ],
        compiler_params=pltpu.CompilerParams(
            collective_id=0, has_side_effects=True, vmem_limit_bytes=58 * 2**20
        ),
    )(
        features.reshape(CELLS, C),
        geometry.reshape(ROWS, WIDTH),
        bc_class,
        code_scale,
        bc_bias,
        kernel_one.reshape(9 * C, HALF),
        kernel_two.reshape(9 * C, HALF),
        cotangent.reshape(CELLS, C),
    )
    factor = 1.0 / math.sqrt(8 * 128 * 256)

    def scaled(g):
        return (g.astype(F32) * factor).reshape(3, 3, C, HALF)

    return grad_features.reshape(features.shape), scaled(g_one), scaled(g_two)


def solution(mesh):
    placed = (
        P(("dp", "fsdp"), "spatial", None, None),
        P(("dp", "fsdp"), "spatial", None),
        P(("dp", "fsdp")),
        P(),
        P(),
        P(None, None, None, "fsdp"),
        P(None, None, None, "fsdp"),
        P(("dp", "fsdp"), "spatial", None, None),
    )
    return jax.shard_map(
        on_device,
        mesh=mesh,
        in_specs=placed,
        out_specs=(
            P(("dp", "fsdp"), "spatial", None, None),
            P(None, None, None, "fsdp"),
            P(None, None, None, "fsdp"),
        ),
        check_vma=False,
    )
```

```python
import functools
import math

import jax
import jax.numpy as jnp
from jax import lax
from jax.experimental import pallas as pl
from jax.experimental.pallas import tpu as pltpu
from jax.sharding import PartitionSpec as P

MESH = pl.DeviceIdType.MESH
BF, F32 = jnp.bfloat16, jnp.float32
ROWS, WIDTH, C, HALF = 8, 256, 256, 128
CELLS = ROWS * WIDTH
QUARTER = 9 * C // 4
NN = (((1,), (0,)), ((), ()))
NT = (((1,), (1,)), ((), ()))
PIECES = 6
LINE_AXIS = ("z", "y", "x", "z", "y", "x")
SLOPE = math.sqrt(2.0 / math.pi)


def dot(a, b, dims):
    return lax.dot_general(a, b, dims, preferred_element_type=F32)


def put_shifted(value, low_ref, mid_ref, high_ref):
    place = lax.broadcasted_iota(jnp.int32, value.shape, 0)
    low_ref[...] = jnp.where(place == 0, 0.0, pltpu.roll(value, 1, 0)).astype(BF)
    mid_ref[...] = value.astype(BF)
    high_ref[...] = jnp.where(place == WIDTH - 1, 0.0, pltpu.roll(value, WIDTH - 1, 0)).astype(BF)


def body(
    feat, geo, bc, scale, bias, k1, k2, cot, gf, g_two, g_one,
    code, fbuf, cbuf, gbuf, geot, sbuf, bbuf, gated_halo, cot_halo, pre_halo, edge,
    xg, xgt, xc, xp, w1, w2, slope, gact, actt, part,
    sib_out, sib_in, plane_out, plane_in, line_out, line_in, shard,
    load_sem, hop_sem, halo_send, halo_recv, w_send, w_recv, r_send, r_recv,
):
    dp = lax.axis_index("dp")
    sp = lax.axis_index("spatial")
    fs = lax.axis_index("fsdp")
    core, cx, yh = sp % 2, (sp // 2) % 4, sp // 8
    cy = yh * 2 + fs
    other = 1 - fs

    xs = [cx] + [(cx + i) % 4 for i in range(1, 4)]
    ys = [cy] + [(cy + i) % 4 for i in range(1, 4)]
    zs = [dp] + [(dp + i) % 4 for i in range(1, 4)]
    y_part = [(y // 2) * 8 + core for y in ys]
    y_fs = [y % 2 for y in ys]

    def device(i, j, k):
        return (zs[k], y_part[j] + 2 * xs[i], y_fs[j])

    sibling = (dp, sp + 1 - 2 * core, fs)
    up, down = (dp, sp - 1, fs), (dp, sp + 1, fs)
    has_up, has_down = sp > 0, sp < 15

    def offset_of(axis, k):
        side, step = k // 4, k % 4
        return {"z": (side, step, 0), "y": (side, 0, step), "x": (0, step, side)}[axis]

    barrier = pltpu.get_barrier_semaphore()

    def greet(target):
        pl.semaphore_signal(barrier, inc=1, device_id=target, device_id_type=MESH)

    ring = []
    for step in (1, 3):
        ring += [device(0, step, 0), device(step, 0, 0), device(0, 0, step)]
    greet(sibling)
    for target in ring:
        greet(target)
    pl.when(jnp.logical_and(core == 0, has_up))(lambda: greet(up))
    pl.when(jnp.logical_and(core == 1, has_down))(lambda: greet(down))

    def tell(n):
        for target in ring:
            pl.semaphore_signal(hop_sem.at[n], inc=1, device_id=target, device_id_type=MESH)

    def heard(n):
        pl.semaphore_wait(hop_sem.at[n], 6)

    def load(src, dst, i):
        cp = pltpu.make_async_copy(src, dst, load_sem.at[i])
        cp.start()
        return cp

    bc_cp = load(bc, code, 7)
    geo_cp = load(geo, gbuf, 0)
    scale_cp = load(scale, sbuf, 1)
    bias_cp = load(bias, bbuf, 2)
    feat_cp = load(feat, fbuf, 3)
    cot_cp = load(cot, cbuf, 4)
    k2_cp = load(k2, w2.at[fs], 5)
    k1_cp = load(k1, w1.at[fs], 6)

    def remote(src, dst, send, recv, target):
        return pltpu.make_async_remote_copy(
            src_ref=src, dst_ref=dst, send_sem=send, recv_sem=recv, device_id=target, device_id_type=MESH
        )

    def halo_up(src, n, buf):
        return remote(src, buf.at[1], halo_send.at[n, 0], halo_recv.at[n, 1], up)

    def halo_down(src, n, buf):
        return remote(src, buf.at[0], halo_send.at[n, 1], halo_recv.at[n, 0], down)

    top, bottom = pl.ds(0, WIDTH), pl.ds(CELLS - WIDTH, WIDTH)
    cot_up = halo_up(cot.at[top], 0, cot_halo)
    cot_down = halo_down(cot.at[bottom], 0, cot_halo)
    gated_up = halo_up(edge.at[0], 1, gated_halo)
    gated_down = halo_down(edge.at[1], 1, gated_halo)
    pre_up = halo_up(xp.at[pl.ds(WIDTH, WIDTH), pl.ds(C, C)], 2, pre_halo)
    pre_down = halo_down(xp.at[pl.ds(CELLS, WIDTH), pl.ds(C, C)], 2, pre_halo)

    next_a = (dp, sp, other)
    next_b = (dp, (1 - yh) * 8 + cx * 2 + core, other)

    def quarter_copies(i, src, w):
        out = []
        for side, target in ((0, next_a), (1, next_b)):
            at = pl.ds(pl.multiple_of((2 * core + side) * QUARTER, 16), QUARTER)
            out.append(remote(src.at[at], w.at[fs, at], w_send.at[i, side], w_recv.at[i, side], target))
        at = pl.ds(pl.multiple_of(2 * core * QUARTER, 16), 2 * QUARTER)
        out.append(remote(w.at[other, at], w.at[other, at], w_send.at[i, 2], w_recv.at[i, 2], sibling))
        return out

    w1_copies = quarter_copies(0, k1, w1)
    w2_copies = quarter_copies(1, k2, w2)

    geo_cp.wait()
    geot[...] = jnp.transpose(gbuf[...])
    scale_cp.wait()
    bias_cp.wait()
    bc_cp.wait()
    classes = lax.broadcasted_iota(jnp.int32, (8, C), 0)
    offset = jnp.sum(jnp.where(classes == code[0], bbuf[...], 0.0), axis=0, keepdims=True)

    def gain_of(row):
        cell = geot[:, row : row + 1]
        return jnp.where(
            cell == 0, sbuf[0:1, :], jnp.where(cell == 1, sbuf[1:2, :], sbuf[2:3, :])
        )

    def put_row(x, r, value):
        at = pl.ds(r * WIDTH, WIDTH)
        put_shifted(value, x.at[at, pl.ds(0, C)], x.at[at, pl.ds(C, C)], x.at[at, pl.ds(2 * C, C)])

    def gated_row(row):
        f = fbuf[row * WIDTH : (row + 1) * WIDTH, :].astype(F32)
        return f * gain_of(row) + offset

    feat_cp.wait()
    for row in (0, 7, 1, 2, 3, 4, 5, 6):
        value = gated_row(row)
        put_row(xg, row + 1, value)
        if row in (0, 7):
            edge[row // 7] = value.astype(BF)

    strangers = jnp.where(core == 0, jnp.where(has_up, 1, 0), jnp.where(has_down, 1, 0))
    pl.semaphore_wait(barrier, 7 + strangers)
    for cp in w1_copies[:2]:
        cp.start()
    pl.when(has_up)(lambda: cot_up.start())
    pl.when(has_down)(lambda: cot_down.start())
    pl.when(has_up)(lambda: gated_up.start())
    pl.when(has_down)(lambda: gated_down.start())
    for cp in w2_copies[:2]:
        cp.start()
    tell(0)

    def put_cot(r, value):
        at = pl.ds(r * WIDTH, WIDTH)
        for h in range(2):
            put_shifted(
                value[:, h * HALF : (h + 1) * HALF],
                xc.at[h, at, pl.ds(0, HALF)],
                xc.at[h, at, pl.ds(HALF, HALF)],
                xc.at[h, at, pl.ds(2 * HALF, HALF)],
            )

    cot_cp.wait()
    for row in range(ROWS):
        put_cot(row + 1, cbuf[row * WIDTH : (row + 1) * WIDTH, :].astype(F32))

    def grad_act_half(h, r, rows):
        lhs = jnp.concatenate([xc[h, pl.ds((r + d) * WIDTH, rows * WIDTH), :] for d in range(3)], axis=1)
        rhs = jnp.concatenate([w2[h, (8 - t) * C : (9 - t) * C, :] for t in range(9)], axis=1)
        return dot(lhs, rhs, NT)

    k2_cp.wait()
    for r in (2, 4):
        gact[r * WIDTH : (r + 2) * WIDTH, :] = grad_act_half(fs, r, 2)

    def halo_rows(up_copy, down_copy, buf, put):
        @pl.when(has_up)
        def _():
            down_copy.wait_recv()
            put(0, buf[0].astype(F32))

        @pl.when(jnp.logical_not(has_up))
        def _():
            put(0, jnp.zeros((WIDTH, C), F32))

        @pl.when(has_down)
        def _():
            up_copy.wait_recv()
            put(ROWS + 1, buf[1].astype(F32))

        @pl.when(jnp.logical_not(has_down))
        def _():
            put(ROWS + 1, jnp.zeros((WIDTH, C), F32))

    heard(0)
    tell(1)
    halo_rows(cot_up, cot_down, cot_halo, put_cot)
    for r in (0, 6):
        gact[r * WIDTH : (r + 2) * WIDTH, :] = grad_act_half(fs, r, 2)

    def turn(r):
        at = pl.ds(r * WIDTH, WIDTH)
        for e in range(3):
            xgt[e * C : (e + 1) * C, at] = jnp.transpose(xg[at, e * C : (e + 1) * C])

    for r in range(1, ROWS + 1):
        turn(r)
    for cp in w1_copies[:2]:
        cp.wait_recv()
    w1_copies[2].start()
    halo_rows(gated_up, gated_down, gated_halo, functools.partial(put_row, xg))
    turn(0)
    turn(ROWS + 1)
    k1_cp.wait()
    w1_copies[2].wait_recv()

    heard(1)
    tell(2)

    def big_lhs(x, r, rows):
        return jnp.concatenate([x[pl.ds((r + d) * WIDTH, rows * WIDTH), :] for d in range(3)], axis=1)

    def act_rows(r):
        v = dot(big_lhs(xg, r, 2), jnp.concatenate([w1[0], w1[1]], axis=1), NN)
        at = slice(r * WIDTH, (r + 2) * WIDTH)
        sq = v * v
        t = jnp.tanh(SLOPE * (v + 0.044715 * (sq * v)))
        half = 0.5 * (1.0 + t)
        slope[at, :] = half + 0.5 * v * (1.0 - t * t) * (SLOPE * (1.0 + (3 * 0.044715) * sq))
        actt[:, at] = jnp.transpose((v * half).astype(BF))

    for r in (0, 2, 4, 6):
        act_rows(r)
    for cp in w2_copies[:2]:
        cp.wait_recv()
    w2_copies[2].start()
    heard(2)

    def sib_copy(p):
        return remote(sib_out.at[p], sib_in.at[p], r_send.at[p, 0], r_recv.at[p, 0], sibling)

    def mine(p, source):
        return source[p, :, pl.ds(pl.multiple_of(core * HALF, HALF), HALF), :]

    def stage1(p):
        sib_out[p] = part[p, :, pl.ds(pl.multiple_of((1 - core) * HALF, HALF), HALF), :].astype(BF)
        sib_copy(p).start()

    def plane_wait(p):
        return remote(plane_in.at[p], plane_in.at[p], r_send.at[p, 1], r_recv.at[p, 1], sibling)

    def slot_of(i, j, k, axis):
        x, y, z = xs[i], ys[j], zs[k]
        return {"z": x * 4 + y, "y": x * 4 + z, "x": z * 4 + y}[axis]

    keeps = dp % 2 == fs

    def stage2(p):
        axis = LINE_AXIS[p]
        sib_copy(p).wait_recv()
        total = mine(p, part) + sib_in[p].astype(F32)
        for block in range(8):
            for h in range(2):
                plane_out[p, block * 2 + h] = total[
                    :, block * 16 : (block + 1) * 16, h * HALF : (h + 1) * HALF
                ].astype(BF)

        for k in range(1, 16):
            to = offset_of(axis, k)
            remote(
                plane_out.at[p, slot_of(*to, axis)], plane_in.at[p, k - 1],
                r_send.at[p, 1], r_recv.at[p, 1], device(*to),
            ).start()

    def line_wait(p):
        return remote(line_in.at[p], line_in.at[p], r_send.at[p, 2], r_recv.at[p, 2], sibling)

    def stage3(p):
        axis = LINE_AXIS[p]
        plane_wait(p).wait_recv()
        total = plane_out[p, slot_of(0, 0, 0, axis)].astype(F32)
        for k in range(15):
            total = total + plane_in[p, k].astype(F32)
        line_out[p] = total.astype(BF)

        for k in range(1, 4):
            to = {"z": (0, 0, k), "y": (0, k, 0), "x": (k, 0, 0)}[axis]

            def go(k=k, to=to):
                remote(line_out.at[p], line_in.at[p, k - 1], r_send.at[p, 2], r_recv.at[p, 2], device(*to)).start()

            if axis == "y":
                pl.when(y_fs[k] == dp % 2)(go)
            else:
                go()

    def row_of(block):
        return pl.ds(pl.multiple_of(core * HALF + block * 16, 16), 16)

    def line_send_wait(p):
        def some(n):
            return remote(line_in.at[p, pl.ds(0, n)], line_in.at[p, pl.ds(0, n)], r_send.at[p, 2], r_recv.at[p, 2], sibling)

        if LINE_AXIS[p] == "y":
            pl.when(keeps)(lambda: some(1).wait_send())
            pl.when(jnp.logical_not(keeps))(lambda: some(2).wait_send())
        else:
            some(3).wait_send()

    def gather_wait(p, n):
        some = plane_in.at[p, pl.ds(0, n)]
        return remote(some, some, r_send.at[p, 3], r_recv.at[p, 3], sibling)

    def gather_recv_wait(p):
        if LINE_AXIS[p] == "y":
            pl.when(keeps)(lambda: gather_wait(p, 7).wait_recv())
            pl.when(jnp.logical_not(keeps))(lambda: gather_wait(p, 8).wait_recv())
        else:
            gather_wait(p, 7).wait_recv()

    def gather_send_wait(p):
        if LINE_AXIS[p] == "y":
            pl.when(keeps)(lambda: gather_wait(p, 15).wait_send())
        else:
            gather_wait(p, 7).wait_send()

    def finish_shard(p):
        axis = LINE_AXIS[p]
        line_wait(p).wait_recv()
        total = line_out[p].astype(F32)
        for k in range(3):
            total = total + line_in[p, k].astype(F32)
        shard[p] = total.astype(BF)
        block = {"z": cx * 2 + yh, "y": cx * 2 + dp // 2, "x": dp * 2 + yh}[axis]
        three = pl.ds(3 * (p % 3), 3)
        grads = (g_two, g_one)[p // 3]
        grads[three, row_of(block), :] = total.astype(BF)

        for k in range(1, 16):
            to = offset_of(axis, k)
            if axis != "y" and to[1] % 2:
                continue
            remote(
                shard.at[p], grads.at[three, row_of(block)], r_send.at[p, 3], r_recv.at[p, 3], device(*to)
            ).start()

    def stage4(p):
        if LINE_AXIS[p] == "y":
            pl.when(keeps)(lambda: finish_shard(p))
        else:
            finish_shard(p)

    def last_copy(p):
        at = (g_two, g_one)[p // 3].at[pl.ds(3 * (p % 3), 3), pl.ds(pl.multiple_of(core * HALF, HALF), HALF)]
        return remote(at, at, r_send.at[p, 4], r_recv.at[p, 4], sibling)

    def stage5(p):
        gather_recv_wait(p)
        last_copy(p).start()

    for d in range(3):
        for e in range(3):
            at, lanes = pl.ds((2 - d) * WIDTH, CELLS), slice((2 - e) * HALF, (3 - e) * HALF)
            part[d, e] = dot(actt[...], jnp.concatenate([xc[0, at, lanes], xc[1, at, lanes]], axis=1), NN)
        stage1(d)
        if d >= 1:
            stage2(d - 1)

    w2_copies[2].wait_recv()

    def grad_pre_rows(r):
        at = slice(r * WIDTH, (r + 2) * WIDTH)
        g = (gact[at, :] + grad_act_half(other, r, 2)) * slope[at, :]
        for i in range(2):
            put_row(xp, r + i + 1, g[i * WIDTH : (i + 1) * WIDTH])

    grad_pre_rows(0)
    pl.when(has_up)(lambda: pre_up.start())
    grad_pre_rows(6)
    pl.when(has_down)(lambda: pre_down.start())
    stage2(2)
    grad_pre_rows(2)
    grad_pre_rows(4)

    for d in range(3):
        p = 3 + d
        three = dot(xgt[:, pl.ds(d * WIDTH, CELLS)], xp[pl.ds(WIDTH, CELLS), C : 2 * C], NN)
        for e in range(3):
            part[p, e] = three[e * C : (e + 1) * C]
        stage1(p)
        if d == 1:
            stage2(3)
        elif d == 2:
            stage2(4)
            stage3(0)

    halo_rows(pre_up, pre_down, pre_halo, functools.partial(put_row, xp))

    def back_rows(r):
        rhs = jnp.concatenate(
            [jnp.concatenate([w1[0, (8 - t) * C : (9 - t) * C, :], w1[1, (8 - t) * C : (9 - t) * C, :]], axis=1) for t in range(9)],
            axis=1,
        )
        g = dot(big_lhs(xp, r, 2), rhs, NT)
        for i in range(2):
            at = slice((r + i) * WIDTH, (r + i + 1) * WIDTH)
            total = cbuf[at, :].astype(F32) + g[i * WIDTH : (i + 1) * WIDTH]
            fbuf[at, :] = (total * gain_of(r + i)).astype(BF)

    back_rows(0)
    stage2(5)
    stage3(1)
    back_rows(2)
    stage3(2)
    back_rows(4)
    stage4(0)
    stage3(3)
    back_rows(6)
    out_cp = pltpu.make_async_copy(fbuf, gf, load_sem.at[3])
    out_cp.start()
    stage4(1)
    stage3(4)
    stage4(2)
    stage3(5)
    stage5(0)
    stage4(3)
    stage5(1)
    stage4(4)
    stage5(2)
    stage4(5)
    stage5(3)
    stage5(4)
    stage5(5)
    for p in range(PIECES):
        last_copy(p).wait_recv()

    for p in range(PIECES):
        sib_copy(p).wait_send()
        plane_wait(p).wait_send()
        line_send_wait(p)
        gather_send_wait(p)
        last_copy(p).wait_send()
    for cp in w1_copies + w2_copies:
        cp.wait_send()
    for ups, downs in ((cot_up, cot_down), (gated_up, gated_down), (pre_up, pre_down)):
        pl.when(has_up)(lambda ups=ups: ups.wait_send())
        pl.when(has_down)(lambda downs=downs: downs.wait_send())
    out_cp.wait()


def on_device(features, geometry, bc_class, code_scale, bc_bias, kernel_one, kernel_two, cotangent):
    any_spec = pl.BlockSpec(memory_space=pl.ANY)
    vmem = pltpu.VMEM
    dma = pltpu.SemaphoreType.DMA
    grad_features, g_two, g_one = pl.pallas_call(
        body,
        out_shape=(
            jax.ShapeDtypeStruct((CELLS, C), BF),
            jax.ShapeDtypeStruct((9, C, HALF), BF),
            jax.ShapeDtypeStruct((9, C, HALF), BF),
        ),
        in_specs=[any_spec] * 8,
        out_specs=(any_spec, pl.BlockSpec(memory_space=pltpu.VMEM), pl.BlockSpec(memory_space=pltpu.VMEM)),
        scratch_shapes=[
            pltpu.SMEM((1,), jnp.int32),
            vmem((CELLS, C), BF),
            vmem((CELLS, C), BF),
            vmem((ROWS, WIDTH), jnp.int32),
            vmem((WIDTH, ROWS), jnp.int32),
            vmem((3, C), F32),
            vmem((8, C), F32),
            vmem((2, WIDTH, C), BF),
            vmem((2, WIDTH, C), BF),
            vmem((2, WIDTH, C), BF),
            vmem((2, WIDTH, C), BF),
            vmem((CELLS + 2 * WIDTH, 3 * C), BF),
            vmem((3 * C, CELLS + 2 * WIDTH), BF),
            vmem((2, CELLS + 2 * WIDTH, 3 * HALF), BF),
            vmem((CELLS + 2 * WIDTH, 3 * C), BF),
            vmem((2, 9 * C, HALF), BF),
            vmem((2, 9 * C, HALF), BF),
            vmem((CELLS, C), F32),
            vmem((CELLS, C), F32),
            vmem((C, CELLS), BF),
            vmem((PIECES, 3, C, C), F32),
            vmem((PIECES, 3, HALF, C), BF),
            vmem((PIECES, 3, HALF, C), BF),
            vmem((PIECES, 16, 3, 16, HALF), BF),
            vmem((PIECES, 15, 3, 16, HALF), BF),
            vmem((PIECES, 3, 16, HALF), BF),
            vmem((PIECES, 3, 3, 16, HALF), BF),
            vmem((PIECES, 3, 16, HALF), BF),
            dma((8,)),
            pltpu.SemaphoreType.REGULAR((3,)),
            dma((3, 2)),
            dma((3, 2)),
            dma((2, 3)),
            dma((2, 3)),
            dma((PIECES, 5)),
            dma((PIECES, 5)),
        ],
        compiler_params=pltpu.CompilerParams(
            collective_id=0, has_side_effects=True, vmem_limit_bytes=58 * 2**20
        ),
    )(
        features.reshape(CELLS, C),
        geometry.reshape(ROWS, WIDTH),
        bc_class,
        code_scale,
        bc_bias,
        kernel_one.reshape(9 * C, HALF),
        kernel_two.reshape(9 * C, HALF),
        cotangent.reshape(CELLS, C),
    )
    factor = 1.0 / math.sqrt(8 * 128 * 256)

    def scaled(g):
        return (g.astype(F32) * factor).reshape(3, 3, C, HALF)

    return grad_features.reshape(features.shape), scaled(g_one), scaled(g_two)


def solution(mesh):
    placed = (
        P(("dp", "fsdp"), "spatial", None, None),
        P(("dp", "fsdp"), "spatial", None),
        P(("dp", "fsdp")),
        P(),
        P(),
        P(None, None, None, "fsdp"),
        P(None, None, None, "fsdp"),
        P(("dp", "fsdp"), "spatial", None, None),
    )
    return jax.shard_map(
        on_device,
        mesh=mesh,
        in_specs=placed,
        out_specs=(
            P(("dp", "fsdp"), "spatial", None, None),
            P(None, None, None, "fsdp"),
            P(None, None, None, "fsdp"),
        ),
        check_vma=False,
    )
```

```python
import functools
import math

import jax
import jax.numpy as jnp
from jax import lax
from jax.experimental import pallas as pl
from jax.experimental.pallas import tpu as pltpu
from jax.sharding import PartitionSpec as P

MESH = pl.DeviceIdType.MESH
BF, F32 = jnp.bfloat16, jnp.float32
ROWS, WIDTH, C, HALF = 8, 256, 256, 128
CELLS = ROWS * WIDTH
QUARTER = 9 * C // 4
NN = (((1,), (0,)), ((), ()))
NT = (((1,), (1,)), ((), ()))
PIECES = 6
LAST = 5
LINE_AXIS = ("z", "y", "x", "z", "y", "x")
SLOPE = math.sqrt(2.0 / math.pi)


def dot(a, b, dims):
    return lax.dot_general(a, b, dims, preferred_element_type=F32)


def put_shifted(value, low_ref, mid_ref, high_ref):
    place = lax.broadcasted_iota(jnp.int32, value.shape, 0)
    low_ref[...] = jnp.where(place == 0, 0.0, pltpu.roll(value, 1, 0)).astype(BF)
    mid_ref[...] = value.astype(BF)
    high_ref[...] = jnp.where(place == WIDTH - 1, 0.0, pltpu.roll(value, WIDTH - 1, 0)).astype(BF)


def body(
    feat, geo, bc, scale, bias, k1, k2, cot, gf, g_two, g_one,
    code, fbuf, cbuf, gbuf, geot, sbuf, bbuf, gated_halo, cot_halo, pre_halo, edge,
    xg, xgt, xc, xp, w1, w2, slope, gact, actt, part,
    sib_out, sib_in, plane_out, plane_in, line_out, line_in, shard, gather_in,
    load_sem, hop_sem, halo_send, halo_recv, w_send, w_recv, r_send, r_recv,
):
    dp = lax.axis_index("dp")
    sp = lax.axis_index("spatial")
    fs = lax.axis_index("fsdp")
    core, cx, yh = sp % 2, (sp // 2) % 4, sp // 8
    cy = yh * 2 + fs
    other = 1 - fs

    xs = [cx] + [(cx + i) % 4 for i in range(1, 4)]
    ys = [cy] + [(cy + i) % 4 for i in range(1, 4)]
    zs = [dp] + [(dp + i) % 4 for i in range(1, 4)]
    y_part = [(y // 2) * 8 + core for y in ys]
    y_fs = [y % 2 for y in ys]

    def device(i, j, k):
        return (zs[k], y_part[j] + 2 * xs[i], y_fs[j])

    def across(i, j, k):
        return (zs[k], y_part[j] + 2 * xs[i] + 1 - 2 * core, y_fs[j])

    sibling = (dp, sp + 1 - 2 * core, fs)
    up, down = (dp, sp - 1, fs), (dp, sp + 1, fs)
    has_up, has_down = sp > 0, sp < 15

    def offset_of(axis, k):
        side, step = k // 4, k % 4
        return {"z": (side, step, 0), "y": (side, 0, step), "x": (0, step, side)}[axis]

    barrier = pltpu.get_barrier_semaphore()

    def greet(target):
        pl.semaphore_signal(barrier, inc=1, device_id=target, device_id_type=MESH)

    ring = []
    for step in (1, 3):
        ring += [device(0, step, 0), device(step, 0, 0), device(0, 0, step)]
    greet(sibling)
    for target in ring:
        greet(target)
    pl.when(jnp.logical_and(core == 0, has_up))(lambda: greet(up))
    pl.when(jnp.logical_and(core == 1, has_down))(lambda: greet(down))

    def tell(n):
        for target in ring:
            pl.semaphore_signal(hop_sem.at[n], inc=1, device_id=target, device_id_type=MESH)

    def heard(n):
        pl.semaphore_wait(hop_sem.at[n], 6)

    def load(src, dst, i):
        cp = pltpu.make_async_copy(src, dst, load_sem.at[i])
        cp.start()
        return cp

    bc_cp = load(bc, code, 7)
    geo_cp = load(geo, gbuf, 0)
    scale_cp = load(scale, sbuf, 1)
    bias_cp = load(bias, bbuf, 2)
    feat_cp = load(feat, fbuf, 3)
    cot_cp = load(cot, cbuf, 4)
    k2_cp = load(k2, w2.at[fs], 5)
    k1_cp = load(k1, w1.at[fs], 6)

    def remote(src, dst, send, recv, target):
        return pltpu.make_async_remote_copy(
            src_ref=src, dst_ref=dst, send_sem=send, recv_sem=recv, device_id=target, device_id_type=MESH
        )

    def halo_up(src, n, buf):
        return remote(src, buf.at[1], halo_send.at[n, 0], halo_recv.at[n, 1], up)

    def halo_down(src, n, buf):
        return remote(src, buf.at[0], halo_send.at[n, 1], halo_recv.at[n, 0], down)

    top, bottom = pl.ds(0, WIDTH), pl.ds(CELLS - WIDTH, WIDTH)
    cot_up = halo_up(cot.at[top], 0, cot_halo)
    cot_down = halo_down(cot.at[bottom], 0, cot_halo)
    gated_up = halo_up(edge.at[0], 1, gated_halo)
    gated_down = halo_down(edge.at[1], 1, gated_halo)
    pre_up = halo_up(xp.at[pl.ds(WIDTH, WIDTH), pl.ds(C, C)], 2, pre_halo)
    pre_down = halo_down(xp.at[pl.ds(CELLS, WIDTH), pl.ds(C, C)], 2, pre_halo)

    next_a = (dp, sp, other)
    next_b = (dp, (1 - yh) * 8 + cx * 2 + core, other)

    def quarter_copies(i, src, w):
        out = []
        for side, target in ((0, next_a), (1, next_b)):
            at = pl.ds(pl.multiple_of((2 * core + side) * QUARTER, 16), QUARTER)
            out.append(remote(src.at[at], w.at[fs, at], w_send.at[i, side], w_recv.at[i, side], target))
        at = pl.ds(pl.multiple_of(2 * core * QUARTER, 16), 2 * QUARTER)
        out.append(remote(w.at[other, at], w.at[other, at], w_send.at[i, 2], w_recv.at[i, 2], sibling))
        return out

    w1_copies = quarter_copies(0, k1, w1)
    w2_copies = quarter_copies(1, k2, w2)

    geo_cp.wait()
    geot[...] = jnp.transpose(gbuf[...])
    scale_cp.wait()
    bias_cp.wait()
    bc_cp.wait()
    classes = lax.broadcasted_iota(jnp.int32, (8, C), 0)
    offset = jnp.sum(jnp.where(classes == code[0], bbuf[...], 0.0), axis=0, keepdims=True)

    def gain_of(row):
        cell = geot[:, row : row + 1]
        return jnp.where(
            cell == 0, sbuf[0:1, :], jnp.where(cell == 1, sbuf[1:2, :], sbuf[2:3, :])
        )

    def put_row(x, r, value):
        at = pl.ds(r * WIDTH, WIDTH)
        put_shifted(value, x.at[at, pl.ds(0, C)], x.at[at, pl.ds(C, C)], x.at[at, pl.ds(2 * C, C)])

    def gated_row(row):
        f = fbuf[row * WIDTH : (row + 1) * WIDTH, :].astype(F32)
        return f * gain_of(row) + offset

    feat_cp.wait()
    for row in (0, 7, 1, 2, 3, 4, 5, 6):
        value = gated_row(row)
        put_row(xg, row + 1, value)
        if row in (0, 7):
            edge[row // 7] = value.astype(BF)

    strangers = jnp.where(core == 0, jnp.where(has_up, 1, 0), jnp.where(has_down, 1, 0))
    pl.semaphore_wait(barrier, 7 + strangers)
    for cp in w1_copies[:2]:
        cp.start()
    pl.when(has_up)(lambda: cot_up.start())
    pl.when(has_down)(lambda: cot_down.start())
    pl.when(has_up)(lambda: gated_up.start())
    pl.when(has_down)(lambda: gated_down.start())
    for cp in w2_copies[:2]:
        cp.start()
    tell(0)

    def put_cot(r, value):
        at = pl.ds(r * WIDTH, WIDTH)
        for h in range(2):
            put_shifted(
                value[:, h * HALF : (h + 1) * HALF],
                xc.at[h, at, pl.ds(0, HALF)],
                xc.at[h, at, pl.ds(HALF, HALF)],
                xc.at[h, at, pl.ds(2 * HALF, HALF)],
            )

    cot_cp.wait()
    for row in range(ROWS):
        put_cot(row + 1, cbuf[row * WIDTH : (row + 1) * WIDTH, :].astype(F32))

    def grad_act_half(h, r, rows):
        lhs = jnp.concatenate([xc[h, pl.ds((r + d) * WIDTH, rows * WIDTH), :] for d in range(3)], axis=1)
        rhs = jnp.concatenate([w2[h, (8 - t) * C : (9 - t) * C, :] for t in range(9)], axis=1)
        return dot(lhs, rhs, NT)

    k2_cp.wait()
    for r in (2, 4):
        gact[r * WIDTH : (r + 2) * WIDTH, :] = grad_act_half(fs, r, 2)

    def halo_rows(up_copy, down_copy, buf, put):
        @pl.when(has_up)
        def _():
            down_copy.wait_recv()
            put(0, buf[0].astype(F32))

        @pl.when(jnp.logical_not(has_up))
        def _():
            put(0, jnp.zeros((WIDTH, C), F32))

        @pl.when(has_down)
        def _():
            up_copy.wait_recv()
            put(ROWS + 1, buf[1].astype(F32))

        @pl.when(jnp.logical_not(has_down))
        def _():
            put(ROWS + 1, jnp.zeros((WIDTH, C), F32))

    def turn(r):
        at = pl.ds(r * WIDTH, WIDTH)
        for e in range(3):
            xgt[e * C : (e + 1) * C, at] = jnp.transpose(xg[at, e * C : (e + 1) * C])

    for r in range(1, ROWS + 1):
        turn(r)
    heard(0)
    tell(1)
    for cp in w1_copies[:2]:
        cp.wait_recv()
    w1_copies[2].start()
    halo_rows(cot_up, cot_down, cot_halo, put_cot)
    for r in (0, 6):
        gact[r * WIDTH : (r + 2) * WIDTH, :] = grad_act_half(fs, r, 2)

    halo_rows(gated_up, gated_down, gated_halo, functools.partial(put_row, xg))
    turn(0)
    turn(ROWS + 1)
    k1_cp.wait()
    w1_copies[2].wait_recv()

    heard(1)
    tell(2)

    def big_lhs(x, r, rows):
        return jnp.concatenate([x[pl.ds((r + d) * WIDTH, rows * WIDTH), :] for d in range(3)], axis=1)

    def act_rows(r):
        v = dot(big_lhs(xg, r, 2), jnp.concatenate([w1[0], w1[1]], axis=1), NN)
        at = slice(r * WIDTH, (r + 2) * WIDTH)
        sq = v * v
        t = jnp.tanh(SLOPE * (v + 0.044715 * (sq * v)))
        half = 0.5 * (1.0 + t)
        slope[at, :] = half + 0.5 * v * (1.0 - t * t) * (SLOPE * (1.0 + (3 * 0.044715) * sq))
        actt[:, at] = jnp.transpose((v * half).astype(BF))

    for r in (0, 2, 4, 6):
        act_rows(r)
    for cp in w2_copies[:2]:
        cp.wait_recv()
    w2_copies[2].start()
    heard(2)
    tell(3)

    def sib_copy(p):
        return remote(sib_out.at[p], sib_in.at[p], r_send.at[p, 0], r_recv.at[p, 0], sibling)

    def mine(p, source):
        return source[p, :, pl.ds(pl.multiple_of(core * HALF, HALF), HALF), :]

    def stage1(p):
        sib_out[p] = part[p, :, pl.ds(pl.multiple_of((1 - core) * HALF, HALF), HALF), :].astype(BF)
        sib_copy(p).start()

    def plane_wait(p):
        return remote(plane_in.at[p], plane_in.at[p], r_send.at[p, 1], r_recv.at[p, 1], sibling)

    def slot_of(i, j, k, axis):
        x, y, z = xs[i], ys[j], zs[k]
        return {"z": x * 4 + y, "y": x * 4 + z, "x": z * 4 + y}[axis]

    keeps = dp % 2 == fs

    def stage2(p):
        axis = LINE_AXIS[p]
        sib_copy(p).wait_recv()
        total = mine(p, part) + sib_in[p].astype(F32)
        for block in range(8):
            for h in range(2):
                plane_out[p, block * 2 + h] = total[
                    :, block * 16 : (block + 1) * 16, h * HALF : (h + 1) * HALF
                ].astype(BF)

        for k in range(1, 16):
            to = offset_of(axis, k)
            remote(
                plane_out.at[p, slot_of(*to, axis)], plane_in.at[p, k - 1],
                r_send.at[p, 1], r_recv.at[p, 1], device(*to),
            ).start()

    def line_wait(p):
        return remote(line_in.at[p], line_in.at[p], r_send.at[p, 2], r_recv.at[p, 2], sibling)

    def stage3(p):
        axis = LINE_AXIS[p]
        plane_wait(p).wait_recv()
        total = plane_out[p, slot_of(0, 0, 0, axis)].astype(F32)
        for k in range(15):
            total = total + plane_in[p, k].astype(F32)
        line_out[p] = total.astype(BF)

        for k in range(1, 4):
            to = {"z": (0, 0, k), "y": (0, k, 0), "x": (k, 0, 0)}[axis]

            def go(k=k, to=to):
                remote(line_out.at[p], line_in.at[p, k - 1], r_send.at[p, 2], r_recv.at[p, 2], device(*to)).start()

            if axis == "y":
                pl.when(y_fs[k] == dp % 2)(go)
            else:
                go()

    def line_send_wait(p):
        def some(n):
            return remote(line_in.at[p, pl.ds(0, n)], line_in.at[p, pl.ds(0, n)], r_send.at[p, 2], r_recv.at[p, 2], sibling)

        if LINE_AXIS[p] == "y":
            pl.when(keeps)(lambda: some(1).wait_send())
            pl.when(jnp.logical_not(keeps))(lambda: some(2).wait_send())
        else:
            some(3).wait_send()

    def gather_wait(p, n):
        some = gather_in.at[p, pl.ds(0, n)]
        return remote(some, some, r_send.at[p, 3], r_recv.at[p, 3], sibling)

    def gather_recv_wait(p):
        if LINE_AXIS[p] == "y":
            pl.when(keeps)(lambda: gather_wait(p, 7).wait_recv())
            pl.when(jnp.logical_not(keeps))(lambda: gather_wait(p, 8).wait_recv())
        else:
            gather_wait(p, 15 if p == LAST else 7).wait_recv()

    def gather_send_wait(p):
        if LINE_AXIS[p] == "y":
            pl.when(keeps)(lambda: gather_wait(p, 15).wait_send())
        else:
            gather_wait(p, 15 if p == LAST else 7).wait_send()

    def gather_list(p):
        offsets = [offset_of(LINE_AXIS[p], k) for k in range(16)]
        if LINE_AXIS[p] != "y":
            offsets = [to for to in offsets if to[1] % 2 == 0]
        return [(to, True) for to in offsets[1:]] + [(to, False) for to in offsets if p == LAST]

    def place(p, value, to, c):
        x, y, z = (of[(4 - step) % 4] for of, step in zip((xs, ys, zs), to, strict=True))
        block = {"z": x * 2 + y // 2, "y": x * 2 + z // 2, "x": z * 2 + y // 2}[LINE_AXIS[p]]
        grads, three = (g_two, g_one)[p // 3], pl.ds(3 * (p % 3), 3)
        grads[three, pl.ds(pl.multiple_of(c * HALF + block * 16, 16), 16), :] = value

    def finish_shard(p):
        axis = LINE_AXIS[p]
        line_wait(p).wait_recv()
        total = line_out[p].astype(F32)
        for k in range(3):
            total = total + line_in[p, k].astype(F32)
        shard[p] = total.astype(BF)
        place(p, total.astype(BF), (0, 0, 0), core)
        for slot, (to, same) in enumerate(gather_list(p)):
            remote(
                shard.at[p], gather_in.at[p, slot], r_send.at[p, 3], r_recv.at[p, 3], device(*to) if same else across(*to)
            ).start()

    def stage4(p):
        if LINE_AXIS[p] == "y":
            pl.when(keeps)(lambda: finish_shard(p))
        else:
            finish_shard(p)

    def last_copy(p):
        at = (g_two, g_one)[p // 3].at[pl.ds(3 * (p % 3), 3), pl.ds(pl.multiple_of(core * HALF, HALF), HALF)]
        return remote(at, at, r_send.at[p, 4], r_recv.at[p, 4], sibling)

    def stage5(p):
        gather_recv_wait(p)
        for slot, (to, same) in enumerate(gather_list(p)):

            def put(slot=slot, to=to, same=same):
                place(p, gather_in[p, slot], to, core if same else 1 - core)

            if LINE_AXIS[p] == "y":
                pl.when(zs[(4 - to[2]) % 4] % 2 == fs)(put)
            else:
                put()
        if p != LAST:
            last_copy(p).start()

    for d in range(3):
        for e in range(3):
            at, lanes = pl.ds((2 - d) * WIDTH, CELLS), slice((2 - e) * HALF, (3 - e) * HALF)
            part[d, e] = dot(actt[...], jnp.concatenate([xc[0, at, lanes], xc[1, at, lanes]], axis=1), NN)
        stage1(d)
        if d >= 1:
            stage2(d - 1)

    heard(3)
    w2_copies[2].wait_recv()

    def grad_pre_rows(r):
        at = slice(r * WIDTH, (r + 2) * WIDTH)
        g = (gact[at, :] + grad_act_half(other, r, 2)) * slope[at, :]
        for i in range(2):
            put_row(xp, r + i + 1, g[i * WIDTH : (i + 1) * WIDTH])

    grad_pre_rows(0)
    pl.when(has_up)(lambda: pre_up.start())
    grad_pre_rows(6)
    pl.when(has_down)(lambda: pre_down.start())
    stage2(2)
    grad_pre_rows(2)
    grad_pre_rows(4)

    for d in range(3):
        p = 3 + d
        three = dot(xgt[:, pl.ds(d * WIDTH, CELLS)], xp[pl.ds(WIDTH, CELLS), C : 2 * C], NN)
        for e in range(3):
            part[p, e] = three[e * C : (e + 1) * C]
        stage1(p)
        if d == 1:
            stage2(3)
        elif d == 2:
            stage2(4)
            stage3(0)

    halo_rows(pre_up, pre_down, pre_halo, functools.partial(put_row, xp))

    def back_rows(r):
        rhs = jnp.concatenate(
            [jnp.concatenate([w1[0, (8 - t) * C : (9 - t) * C, :], w1[1, (8 - t) * C : (9 - t) * C, :]], axis=1) for t in range(9)],
            axis=1,
        )
        g = dot(big_lhs(xp, r, 2), rhs, NT)
        for i in range(2):
            at = slice((r + i) * WIDTH, (r + i + 1) * WIDTH)
            total = cbuf[at, :].astype(F32) + g[i * WIDTH : (i + 1) * WIDTH]
            fbuf[at, :] = (total * gain_of(r + i)).astype(BF)

    back_rows(0)
    stage2(5)
    stage3(1)
    back_rows(2)
    stage3(2)
    back_rows(4)
    stage4(0)
    stage3(3)
    back_rows(6)
    out_cp = pltpu.make_async_copy(fbuf, gf, load_sem.at[3])
    out_cp.start()
    stage4(1)
    stage3(4)
    stage4(2)
    stage3(5)
    stage5(0)
    stage4(3)
    stage5(1)
    stage4(4)
    stage5(2)
    stage4(5)
    stage5(3)
    stage5(4)
    stage5(5)
    for p in range(LAST):
        last_copy(p).wait_recv()

    for p in range(PIECES):
        sib_copy(p).wait_send()
        plane_wait(p).wait_send()
        line_send_wait(p)
        gather_send_wait(p)
        if p != LAST:
            last_copy(p).wait_send()
    for cp in w1_copies + w2_copies:
        cp.wait_send()
    for ups, downs in ((cot_up, cot_down), (gated_up, gated_down), (pre_up, pre_down)):
        pl.when(has_up)(lambda ups=ups: ups.wait_send())
        pl.when(has_down)(lambda downs=downs: downs.wait_send())
    out_cp.wait()


def finish(gf, g_two, g_one, gf_out, two_out, one_out, raw, wide, held, sem):
    factor = 1.0 / math.sqrt(8 * 128 * 256)
    loads, stores = [], []
    for n in range(6):
        src, dst = ((g_two, two_out), (g_one, one_out))[n // 3]
        at = pl.ds(3 * (n % 3), 3)
        loads.append(pltpu.make_async_copy(src.at[at], raw.at[n], sem.at[n]))
        stores.append(pltpu.make_async_copy(wide.at[n], dst.at[at], sem.at[6 + n]))
    for cp in loads:
        cp.start()
    halves = [pl.ds(n * CELLS // 2, CELLS // 2) for n in range(2)]
    ins = [pltpu.make_async_copy(gf.at[at], held.at[at], sem.at[12 + n]) for n, at in enumerate(halves)]
    outs = [pltpu.make_async_copy(held.at[at], gf_out.at[at], sem.at[14 + n]) for n, at in enumerate(halves)]
    for cp in ins:
        cp.start()
    for n in range(6):
        loads[n].wait()
        wide[n] = raw[n].astype(F32) * factor
        stores[n].start()
        if n in (2, 5):
            ins[n // 3].wait()
            outs[n // 3].start()
    for cp in stores + outs:
        cp.wait()


def on_device(features, geometry, bc_class, code_scale, bc_bias, kernel_one, kernel_two, cotangent):
    any_spec = pl.BlockSpec(memory_space=pl.ANY)
    vmem = pltpu.VMEM
    dma = pltpu.SemaphoreType.DMA
    grad_features, g_two, g_one = pl.pallas_call(
        body,
        out_shape=(
            jax.ShapeDtypeStruct((CELLS, C), BF),
            jax.ShapeDtypeStruct((9, C, HALF), BF),
            jax.ShapeDtypeStruct((9, C, HALF), BF),
        ),
        in_specs=[any_spec] * 8,
        out_specs=(any_spec, pl.BlockSpec(memory_space=pltpu.VMEM), pl.BlockSpec(memory_space=pltpu.VMEM)),
        scratch_shapes=[
            pltpu.SMEM((1,), jnp.int32),
            vmem((CELLS, C), BF),
            vmem((CELLS, C), BF),
            vmem((ROWS, WIDTH), jnp.int32),
            vmem((WIDTH, ROWS), jnp.int32),
            vmem((3, C), F32),
            vmem((8, C), F32),
            vmem((2, WIDTH, C), BF),
            vmem((2, WIDTH, C), BF),
            vmem((2, WIDTH, C), BF),
            vmem((2, WIDTH, C), BF),
            vmem((CELLS + 2 * WIDTH, 3 * C), BF),
            vmem((3 * C, CELLS + 2 * WIDTH), BF),
            vmem((2, CELLS + 2 * WIDTH, 3 * HALF), BF),
            vmem((CELLS + 2 * WIDTH, 3 * C), BF),
            vmem((2, 9 * C, HALF), BF),
            vmem((2, 9 * C, HALF), BF),
            vmem((CELLS, C), F32),
            vmem((CELLS, C), F32),
            vmem((C, CELLS), BF),
            vmem((PIECES, 3, C, C), F32),
            vmem((PIECES, 3, HALF, C), BF),
            vmem((PIECES, 3, HALF, C), BF),
            vmem((PIECES, 16, 3, 16, HALF), BF),
            vmem((PIECES, 15, 3, 16, HALF), BF),
            vmem((PIECES, 3, 16, HALF), BF),
            vmem((PIECES, 3, 3, 16, HALF), BF),
            vmem((PIECES, 3, 16, HALF), BF),
            vmem((PIECES, 15, 3, 16, HALF), BF),
            dma((8,)),
            pltpu.SemaphoreType.REGULAR((4,)),
            dma((3, 2)),
            dma((3, 2)),
            dma((2, 3)),
            dma((2, 3)),
            dma((PIECES, 5)),
            dma((PIECES, 5)),
        ],
        compiler_params=pltpu.CompilerParams(
            collective_id=0, has_side_effects=True, vmem_limit_bytes=58 * 2**20
        ),
    )(
        features.reshape(CELLS, C),
        geometry.reshape(ROWS, WIDTH),
        bc_class,
        code_scale,
        bc_bias,
        kernel_one.reshape(9 * C, HALF),
        kernel_two.reshape(9 * C, HALF),
        cotangent.reshape(CELLS, C),
    )
    grad_features, two, one = pl.pallas_call(
        finish,
        out_shape=(
            jax.ShapeDtypeStruct((CELLS, C), BF),
            jax.ShapeDtypeStruct((9, C, HALF), F32),
            jax.ShapeDtypeStruct((9, C, HALF), F32),
        ),
        in_specs=[any_spec] * 3,
        out_specs=(any_spec, any_spec, any_spec),
        scratch_shapes=[vmem((6, 3, C, HALF), BF), vmem((6, 3, C, HALF), F32), vmem((CELLS, C), BF), dma((16,))],
        compiler_params=pltpu.CompilerParams(vmem_limit_bytes=58 * 2**20),
    )(grad_features, g_two, g_one)
    shape = (3, 3, C, HALF)
    return grad_features.reshape(features.shape), one.reshape(shape), two.reshape(shape)


def solution(mesh):
    placed = (
        P(("dp", "fsdp"), "spatial", None, None),
        P(("dp", "fsdp"), "spatial", None),
        P(("dp", "fsdp")),
        P(),
        P(),
        P(None, None, None, "fsdp"),
        P(None, None, None, "fsdp"),
        P(("dp", "fsdp"), "spatial", None, None),
    )
    return jax.shard_map(
        on_device,
        mesh=mesh,
        in_specs=placed,
        out_specs=(
            P(("dp", "fsdp"), "spatial", None, None),
            P(None, None, None, "fsdp"),
            P(None, None, None, "fsdp"),
        ),
        check_vma=False,
    )
```

```python
import functools
import math

import jax
import jax.numpy as jnp
from jax import lax
from jax.experimental import pallas as pl
from jax.experimental.pallas import tpu as pltpu
from jax.sharding import PartitionSpec as P

MESH = pl.DeviceIdType.MESH
BF, F32 = jnp.bfloat16, jnp.float32
ROWS, WIDTH, C, HALF = 8, 256, 256, 128
CELLS = ROWS * WIDTH
QUARTER = 9 * C // 4
NN = (((1,), (0,)), ((), ()))
NT = (((1,), (1,)), ((), ()))
PIECES = 6
LAST = 5
LINE_AXIS = ("z", "y", "x", "z", "y", "x")
SLOPE = math.sqrt(2.0 / math.pi)


def dot(a, b, dims):
    return lax.dot_general(a, b, dims, preferred_element_type=F32)


def put_shifted(value, low_ref, mid_ref, high_ref):
    place = lax.broadcasted_iota(jnp.int32, value.shape, 0)
    low_ref[...] = jnp.where(place == 0, 0.0, pltpu.roll(value, 1, 0)).astype(BF)
    mid_ref[...] = value.astype(BF)
    high_ref[...] = jnp.where(place == WIDTH - 1, 0.0, pltpu.roll(value, WIDTH - 1, 0)).astype(BF)


def body(
    feat, geo, bc, scale, bias, k1, k2, cot, gf, g_two, g_one,
    code, fbuf, cbuf, gbuf, geot, sbuf, bbuf, gated_halo, cot_halo, pre_halo, edge,
    xg, xgt, xc, xp, w1, w2, slope, gact, actt, part,
    sib_out, sib_in, plane_out, plane_in, line_out, line_in, shard, gather_in,
    load_sem, hop_sem, halo_send, halo_recv, w_send, w_recv, r_send, r_recv,
):
    dp = lax.axis_index("dp")
    sp = lax.axis_index("spatial")
    fs = lax.axis_index("fsdp")
    core, cx, yh = sp % 2, (sp // 2) % 4, sp // 8
    cy = yh * 2 + fs
    other = 1 - fs

    xs = [cx] + [(cx + i) % 4 for i in range(1, 4)]
    ys = [cy] + [(cy + i) % 4 for i in range(1, 4)]
    zs = [dp] + [(dp + i) % 4 for i in range(1, 4)]
    y_part = [(y // 2) * 8 + core for y in ys]
    y_fs = [y % 2 for y in ys]

    def device(i, j, k):
        return (zs[k], y_part[j] + 2 * xs[i], y_fs[j])

    def across(i, j, k):
        return (zs[k], y_part[j] + 2 * xs[i] + 1 - 2 * core, y_fs[j])

    sibling = (dp, sp + 1 - 2 * core, fs)
    up, down = (dp, sp - 1, fs), (dp, sp + 1, fs)
    has_up, has_down = sp > 0, sp < 15

    def offset_of(axis, k):
        side, step = k // 4, k % 4
        return {"z": (side, step, 0), "y": (side, 0, step), "x": (0, step, side)}[axis]

    barrier = pltpu.get_barrier_semaphore()

    def greet(target):
        pl.semaphore_signal(barrier, inc=1, device_id=target, device_id_type=MESH)

    ring = []
    for step in (1, 3):
        ring += [device(0, step, 0), device(step, 0, 0), device(0, 0, step)]
    greet(sibling)
    for target in ring:
        greet(target)
    pl.when(jnp.logical_and(core == 0, has_up))(lambda: greet(up))
    pl.when(jnp.logical_and(core == 1, has_down))(lambda: greet(down))

    def tell(n):
        for target in ring:
            pl.semaphore_signal(hop_sem.at[n], inc=1, device_id=target, device_id_type=MESH)

    def heard(n):
        pl.semaphore_wait(hop_sem.at[n], 6)

    def load(src, dst, i):
        cp = pltpu.make_async_copy(src, dst, load_sem.at[i])
        cp.start()
        return cp

    bc_cp = load(bc, code, 7)
    geo_cp = load(geo, gbuf, 0)
    scale_cp = load(scale, sbuf, 1)
    bias_cp = load(bias, bbuf, 2)
    feat_cp = load(feat, fbuf, 3)
    cot_cp = load(cot, cbuf, 4)
    k2_cp = load(k2, w2.at[fs], 5)
    k1_cp = load(k1, w1.at[fs], 6)

    def remote(src, dst, send, recv, target):
        return pltpu.make_async_remote_copy(
            src_ref=src, dst_ref=dst, send_sem=send, recv_sem=recv, device_id=target, device_id_type=MESH
        )

    def halo_up(src, n, buf):
        return remote(src, buf.at[1], halo_send.at[n, 0], halo_recv.at[n, 1], up)

    def halo_down(src, n, buf):
        return remote(src, buf.at[0], halo_send.at[n, 1], halo_recv.at[n, 0], down)

    top, bottom = pl.ds(0, WIDTH), pl.ds(CELLS - WIDTH, WIDTH)
    cot_up = halo_up(cot.at[top], 0, cot_halo)
    cot_down = halo_down(cot.at[bottom], 0, cot_halo)
    gated_up = halo_up(edge.at[0], 1, gated_halo)
    gated_down = halo_down(edge.at[1], 1, gated_halo)
    pre_up = halo_up(xp.at[pl.ds(WIDTH, WIDTH), pl.ds(C, C)], 2, pre_halo)
    pre_down = halo_down(xp.at[pl.ds(CELLS, WIDTH), pl.ds(C, C)], 2, pre_halo)

    next_a = (dp, sp, other)
    next_b = (dp, (1 - yh) * 8 + cx * 2 + core, other)

    def quarter_copies(i, src, w):
        out = []
        for side, target in ((0, next_a), (1, next_b)):
            at = pl.ds(pl.multiple_of((2 * core + side) * QUARTER, 16), QUARTER)
            out.append(remote(src.at[at], w.at[fs, at], w_send.at[i, side], w_recv.at[i, side], target))
        at = pl.ds(pl.multiple_of(2 * core * QUARTER, 16), 2 * QUARTER)
        out.append(remote(w.at[other, at], w.at[other, at], w_send.at[i, 2], w_recv.at[i, 2], sibling))
        return out

    w1_copies = quarter_copies(0, k1, w1)
    w2_copies = quarter_copies(1, k2, w2)

    geo_cp.wait()
    geot[...] = jnp.transpose(gbuf[...])
    scale_cp.wait()
    bias_cp.wait()
    bc_cp.wait()
    classes = lax.broadcasted_iota(jnp.int32, (8, C), 0)
    offset = jnp.sum(jnp.where(classes == code[0], bbuf[...], 0.0), axis=0, keepdims=True)

    def gain_of(row):
        cell = geot[:, row : row + 1]
        return jnp.where(
            cell == 0, sbuf[0:1, :], jnp.where(cell == 1, sbuf[1:2, :], sbuf[2:3, :])
        )

    def put_row(x, r, value):
        at = pl.ds(r * WIDTH, WIDTH)
        put_shifted(value, x.at[at, pl.ds(0, C)], x.at[at, pl.ds(C, C)], x.at[at, pl.ds(2 * C, C)])

    def gated_row(row):
        f = fbuf[row * WIDTH : (row + 1) * WIDTH, :].astype(F32)
        return f * gain_of(row) + offset

    feat_cp.wait()
    for row in (0, 7, 1, 2, 3, 4, 5, 6):
        value = gated_row(row)
        put_row(xg, row + 1, value)
        if row in (0, 7):
            edge[row // 7] = value.astype(BF)

    strangers = jnp.where(core == 0, jnp.where(has_up, 1, 0), jnp.where(has_down, 1, 0))
    pl.semaphore_wait(barrier, 7 + strangers)
    for cp in w1_copies[:2]:
        cp.start()
    pl.when(has_up)(lambda: cot_up.start())
    pl.when(has_down)(lambda: cot_down.start())
    pl.when(has_up)(lambda: gated_up.start())
    pl.when(has_down)(lambda: gated_down.start())
    for cp in w2_copies[:2]:
        cp.start()
    tell(0)

    def put_cot(r, value):
        at = pl.ds(r * WIDTH, WIDTH)
        for h in range(2):
            put_shifted(
                value[:, h * HALF : (h + 1) * HALF],
                xc.at[h, at, pl.ds(0, HALF)],
                xc.at[h, at, pl.ds(HALF, HALF)],
                xc.at[h, at, pl.ds(2 * HALF, HALF)],
            )

    cot_cp.wait()
    for row in range(ROWS):
        put_cot(row + 1, cbuf[row * WIDTH : (row + 1) * WIDTH, :].astype(F32))

    def grad_act_half(h, r, rows):
        lhs = jnp.concatenate([xc[h, pl.ds((r + d) * WIDTH, rows * WIDTH), :] for d in range(3)], axis=1)
        rhs = jnp.concatenate([w2[h, (8 - t) * C : (9 - t) * C, :] for t in range(9)], axis=1)
        return dot(lhs, rhs, NT)

    k2_cp.wait()
    for r in (2, 4):
        gact[r * WIDTH : (r + 2) * WIDTH, :] = grad_act_half(fs, r, 2)

    def halo_rows(up_copy, down_copy, buf, put):
        @pl.when(has_up)
        def _():
            down_copy.wait_recv()
            put(0, buf[0].astype(F32))

        @pl.when(jnp.logical_not(has_up))
        def _():
            put(0, jnp.zeros((WIDTH, C), F32))

        @pl.when(has_down)
        def _():
            up_copy.wait_recv()
            put(ROWS + 1, buf[1].astype(F32))

        @pl.when(jnp.logical_not(has_down))
        def _():
            put(ROWS + 1, jnp.zeros((WIDTH, C), F32))

    def turn(r):
        at = pl.ds(r * WIDTH, WIDTH)
        for e in range(3):
            xgt[e * C : (e + 1) * C, at] = jnp.transpose(xg[at, e * C : (e + 1) * C])

    for r in range(1, ROWS + 1):
        turn(r)
    heard(0)
    tell(1)
    for cp in w1_copies[:2]:
        cp.wait_recv()
    w1_copies[2].start()
    halo_rows(cot_up, cot_down, cot_halo, put_cot)
    for r in (0, 6):
        gact[r * WIDTH : (r + 2) * WIDTH, :] = grad_act_half(fs, r, 2)

    halo_rows(gated_up, gated_down, gated_halo, functools.partial(put_row, xg))
    turn(0)
    turn(ROWS + 1)
    k1_cp.wait()
    w1_copies[2].wait_recv()

    heard(1)
    tell(2)

    def big_lhs(x, r, rows):
        return jnp.concatenate([x[pl.ds((r + d) * WIDTH, rows * WIDTH), :] for d in range(3)], axis=1)

    def act_rows(r):
        v = dot(big_lhs(xg, r, 2), jnp.concatenate([w1[0], w1[1]], axis=1), NN)
        at = slice(r * WIDTH, (r + 2) * WIDTH)
        sq = v * v
        t = jnp.tanh(SLOPE * (v + 0.044715 * (sq * v)))
        half = 0.5 * (1.0 + t)
        slope[at, :] = half + 0.5 * v * (1.0 - t * t) * (SLOPE * (1.0 + (3 * 0.044715) * sq))
        actt[:, at] = jnp.transpose((v * half).astype(BF))

    for r in (0, 2, 4, 6):
        act_rows(r)
    for cp in w2_copies[:2]:
        cp.wait_recv()
    w2_copies[2].start()
    heard(2)
    tell(3)

    def sib_copy(p):
        return remote(sib_out.at[p], sib_in.at[p], r_send.at[p, 0], r_recv.at[p, 0], sibling)

    def mine(p, source):
        return source[p, :, pl.ds(pl.multiple_of(core * HALF, HALF), HALF), :]

    def stage1(p):
        sib_out[p] = part[p, :, pl.ds(pl.multiple_of((1 - core) * HALF, HALF), HALF), :].astype(BF)
        sib_copy(p).start()

    def plane_wait(p):
        return remote(plane_in.at[p], plane_in.at[p], r_send.at[p, 1], r_recv.at[p, 1], sibling)

    def slot_of(i, j, k, axis):
        x, y, z = xs[i], ys[j], zs[k]
        return {"z": x * 4 + y, "y": x * 4 + z, "x": z * 4 + y}[axis]

    keeps = dp % 2 == fs

    def stage2(p):
        axis = LINE_AXIS[p]
        sib_copy(p).wait_recv()
        total = mine(p, part) + sib_in[p].astype(F32)
        for block in range(8):
            for h in range(2):
                plane_out[p, block * 2 + h] = total[
                    :, block * 16 : (block + 1) * 16, h * HALF : (h + 1) * HALF
                ].astype(BF)

        for k in range(1, 16):
            to = offset_of(axis, k)
            remote(
                plane_out.at[p, slot_of(*to, axis)], plane_in.at[p, k - 1],
                r_send.at[p, 1], r_recv.at[p, 1], device(*to),
            ).start()

    def line_wait(p):
        return remote(line_in.at[p], line_in.at[p], r_send.at[p, 2], r_recv.at[p, 2], sibling)

    def stage3(p):
        axis = LINE_AXIS[p]
        plane_wait(p).wait_recv()
        total = plane_out[p, slot_of(0, 0, 0, axis)].astype(F32)
        for k in range(15):
            total = total + plane_in[p, k].astype(F32)
        line_out[p] = total.astype(BF)

        for k in range(1, 4):
            to = {"z": (0, 0, k), "y": (0, k, 0), "x": (k, 0, 0)}[axis]

            def go(k=k, to=to):
                remote(line_out.at[p], line_in.at[p, k - 1], r_send.at[p, 2], r_recv.at[p, 2], device(*to)).start()

            if axis == "y":
                pl.when(y_fs[k] == dp % 2)(go)
            else:
                go()

    def line_send_wait(p):
        def some(n):
            return remote(line_in.at[p, pl.ds(0, n)], line_in.at[p, pl.ds(0, n)], r_send.at[p, 2], r_recv.at[p, 2], sibling)

        if LINE_AXIS[p] == "y":
            pl.when(keeps)(lambda: some(1).wait_send())
            pl.when(jnp.logical_not(keeps))(lambda: some(2).wait_send())
        else:
            some(3).wait_send()

    def gather_wait(p, n):
        some = gather_in.at[p, pl.ds(0, n)]
        return remote(some, some, r_send.at[p, 3], r_recv.at[p, 3], sibling)

    def gather_recv_wait(p):
        if LINE_AXIS[p] == "y":
            pl.when(keeps)(lambda: gather_wait(p, 7).wait_recv())
            pl.when(jnp.logical_not(keeps))(lambda: gather_wait(p, 8).wait_recv())
        else:
            gather_wait(p, 15 if p == LAST else 7).wait_recv()

    def gather_send_wait(p):
        if LINE_AXIS[p] == "y":
            pl.when(keeps)(lambda: gather_wait(p, 15).wait_send())
        else:
            gather_wait(p, 15 if p == LAST else 7).wait_send()

    def gather_list(p):
        offsets = [offset_of(LINE_AXIS[p], k) for k in range(16)]
        if LINE_AXIS[p] != "y":
            offsets = [to for to in offsets if to[1] % 2 == 0]
        return [(to, True) for to in offsets[1:]] + [(to, False) for to in offsets if p == LAST]

    def place(p, value, to, c):
        x, y, z = (of[(4 - step) % 4] for of, step in zip((xs, ys, zs), to, strict=True))
        block = {"z": x * 2 + y // 2, "y": x * 2 + z // 2, "x": z * 2 + y // 2}[LINE_AXIS[p]]
        grads, three = (g_two, g_one)[p // 3], pl.ds(3 * (p % 3), 3)
        grads[three, pl.ds(pl.multiple_of(c * HALF + block * 16, 16), 16), :] = value

    def finish_shard(p):
        axis = LINE_AXIS[p]
        line_wait(p).wait_recv()
        total = line_out[p].astype(F32)
        for k in range(3):
            total = total + line_in[p, k].astype(F32)
        shard[p] = total.astype(BF)
        place(p, total.astype(BF), (0, 0, 0), core)
        for slot, (to, same) in enumerate(gather_list(p)):
            remote(
                shard.at[p], gather_in.at[p, slot], r_send.at[p, 3], r_recv.at[p, 3], device(*to) if same else across(*to)
            ).start()

    def stage4(p):
        if LINE_AXIS[p] == "y":
            pl.when(keeps)(lambda: finish_shard(p))
        else:
            finish_shard(p)

    def last_copy(p):
        at = (g_two, g_one)[p // 3].at[pl.ds(3 * (p % 3), 3), pl.ds(pl.multiple_of(core * HALF, HALF), HALF)]
        return remote(at, at, r_send.at[p, 4], r_recv.at[p, 4], sibling)

    def stage5(p):
        gather_recv_wait(p)
        for slot, (to, same) in enumerate(gather_list(p)):

            def put(slot=slot, to=to, same=same):
                place(p, gather_in[p, slot], to, core if same else 1 - core)

            if LINE_AXIS[p] == "y":
                pl.when(zs[(4 - to[2]) % 4] % 2 == fs)(put)
            else:
                put()
        if p != LAST:
            last_copy(p).start()

    for d in range(3):
        for e in range(3):
            at, lanes = pl.ds((2 - d) * WIDTH, CELLS), slice((2 - e) * HALF, (3 - e) * HALF)
            part[d, e] = dot(actt[...], jnp.concatenate([xc[0, at, lanes], xc[1, at, lanes]], axis=1), NN)
        stage1(d)
        if d >= 1:
            stage2(d - 1)

    heard(3)
    w2_copies[2].wait_recv()

    def grad_pre_rows(r):
        at = slice(r * WIDTH, (r + 2) * WIDTH)
        g = (gact[at, :] + grad_act_half(other, r, 2)) * slope[at, :]
        for i in range(2):
            put_row(xp, r + i + 1, g[i * WIDTH : (i + 1) * WIDTH])

    grad_pre_rows(0)
    pl.when(has_up)(lambda: pre_up.start())
    grad_pre_rows(6)
    pl.when(has_down)(lambda: pre_down.start())
    stage2(2)
    grad_pre_rows(2)
    grad_pre_rows(4)

    for d in range(3):
        p = 3 + d
        three = dot(xgt[:, pl.ds(d * WIDTH, CELLS)], xp[pl.ds(WIDTH, CELLS), C : 2 * C], NN)
        for e in range(3):
            part[p, e] = three[e * C : (e + 1) * C]
        stage1(p)
        if d == 1:
            stage2(3)
        elif d == 2:
            stage2(4)
            stage3(0)

    halo_rows(pre_up, pre_down, pre_halo, functools.partial(put_row, xp))

    def back_rows(r):
        rhs = jnp.concatenate(
            [jnp.concatenate([w1[0, (8 - t) * C : (9 - t) * C, :], w1[1, (8 - t) * C : (9 - t) * C, :]], axis=1) for t in range(9)],
            axis=1,
        )
        g = dot(big_lhs(xp, r, 2), rhs, NT)
        for i in range(2):
            at = slice((r + i) * WIDTH, (r + i + 1) * WIDTH)
            total = cbuf[at, :].astype(F32) + g[i * WIDTH : (i + 1) * WIDTH]
            fbuf[at, :] = (total * gain_of(r + i)).astype(BF)

    back_rows(0)
    stage2(5)
    stage3(1)
    back_rows(2)
    stage3(2)
    back_rows(4)
    stage4(0)
    stage3(3)
    back_rows(6)
    out_cp = pltpu.make_async_copy(fbuf, gf, load_sem.at[3])
    out_cp.start()
    stage3(4)
    stage3(5)
    stage4(1)
    stage4(2)
    stage4(3)
    stage4(4)
    stage4(5)
    stage5(0)
    stage5(1)
    stage5(2)
    stage5(3)
    stage5(4)
    stage5(5)
    for p in range(LAST):
        last_copy(p).wait_recv()

    for p in range(PIECES):
        sib_copy(p).wait_send()
        plane_wait(p).wait_send()
        line_send_wait(p)
        gather_send_wait(p)
        if p != LAST:
            last_copy(p).wait_send()
    for cp in w1_copies + w2_copies:
        cp.wait_send()
    for ups, downs in ((cot_up, cot_down), (gated_up, gated_down), (pre_up, pre_down)):
        pl.when(has_up)(lambda ups=ups: ups.wait_send())
        pl.when(has_down)(lambda downs=downs: downs.wait_send())
    out_cp.wait()


def finish(gf, g_two, g_one, gf_out, two_out, one_out, raw, wide, held, sem):
    factor = 1.0 / math.sqrt(8 * 128 * 256)
    loads, stores = [], []
    for n in range(6):
        src, dst = ((g_two, two_out), (g_one, one_out))[n // 3]
        at = pl.ds(3 * (n % 3), 3)
        loads.append(pltpu.make_async_copy(src.at[at], raw.at[n], sem.at[n]))
        stores.append(pltpu.make_async_copy(wide.at[n], dst.at[at], sem.at[6 + n]))
    for cp in loads:
        cp.start()
    halves = [pl.ds(n * CELLS // 2, CELLS // 2) for n in range(2)]
    ins = [pltpu.make_async_copy(gf.at[at], held.at[at], sem.at[12 + n]) for n, at in enumerate(halves)]
    outs = [pltpu.make_async_copy(held.at[at], gf_out.at[at], sem.at[14 + n]) for n, at in enumerate(halves)]
    for cp in ins:
        cp.start()
    for n in range(6):
        loads[n].wait()
        wide[n] = raw[n].astype(F32) * factor
        stores[n].start()
        if n in (2, 5):
            ins[n // 3].wait()
            outs[n // 3].start()
    for cp in stores + outs:
        cp.wait()


def on_device(features, geometry, bc_class, code_scale, bc_bias, kernel_one, kernel_two, cotangent):
    any_spec = pl.BlockSpec(memory_space=pl.ANY)
    vmem = pltpu.VMEM
    dma = pltpu.SemaphoreType.DMA
    grad_features, g_two, g_one = pl.pallas_call(
        body,
        out_shape=(
            jax.ShapeDtypeStruct((CELLS, C), BF),
            jax.ShapeDtypeStruct((9, C, HALF), BF),
            jax.ShapeDtypeStruct((9, C, HALF), BF),
        ),
        in_specs=[any_spec] * 8,
        out_specs=(any_spec, pl.BlockSpec(memory_space=pltpu.VMEM), pl.BlockSpec(memory_space=pltpu.VMEM)),
        scratch_shapes=[
            pltpu.SMEM((1,), jnp.int32),
            vmem((CELLS, C), BF),
            vmem((CELLS, C), BF),
            vmem((ROWS, WIDTH), jnp.int32),
            vmem((WIDTH, ROWS), jnp.int32),
            vmem((3, C), F32),
            vmem((8, C), F32),
            vmem((2, WIDTH, C), BF),
            vmem((2, WIDTH, C), BF),
            vmem((2, WIDTH, C), BF),
            vmem((2, WIDTH, C), BF),
            vmem((CELLS + 2 * WIDTH, 3 * C), BF),
            vmem((3 * C, CELLS + 2 * WIDTH), BF),
            vmem((2, CELLS + 2 * WIDTH, 3 * HALF), BF),
            vmem((CELLS + 2 * WIDTH, 3 * C), BF),
            vmem((2, 9 * C, HALF), BF),
            vmem((2, 9 * C, HALF), BF),
            vmem((CELLS, C), F32),
            vmem((CELLS, C), F32),
            vmem((C, CELLS), BF),
            vmem((PIECES, 3, C, C), F32),
            vmem((PIECES, 3, HALF, C), BF),
            vmem((PIECES, 3, HALF, C), BF),
            vmem((PIECES, 16, 3, 16, HALF), BF),
            vmem((PIECES, 15, 3, 16, HALF), BF),
            vmem((PIECES, 3, 16, HALF), BF),
            vmem((PIECES, 3, 3, 16, HALF), BF),
            vmem((PIECES, 3, 16, HALF), BF),
            vmem((PIECES, 15, 3, 16, HALF), BF),
            dma((8,)),
            pltpu.SemaphoreType.REGULAR((4,)),
            dma((3, 2)),
            dma((3, 2)),
            dma((2, 3)),
            dma((2, 3)),
            dma((PIECES, 5)),
            dma((PIECES, 5)),
        ],
        compiler_params=pltpu.CompilerParams(
            collective_id=0, has_side_effects=True, vmem_limit_bytes=58 * 2**20
        ),
    )(
        features.reshape(CELLS, C),
        geometry.reshape(ROWS, WIDTH),
        bc_class,
        code_scale,
        bc_bias,
        kernel_one.reshape(9 * C, HALF),
        kernel_two.reshape(9 * C, HALF),
        cotangent.reshape(CELLS, C),
    )
    grad_features, two, one = pl.pallas_call(
        finish,
        out_shape=(
            jax.ShapeDtypeStruct((CELLS, C), BF),
            jax.ShapeDtypeStruct((9, C, HALF), F32),
            jax.ShapeDtypeStruct((9, C, HALF), F32),
        ),
        in_specs=[any_spec] * 3,
        out_specs=(any_spec, any_spec, any_spec),
        scratch_shapes=[vmem((6, 3, C, HALF), BF), vmem((6, 3, C, HALF), F32), vmem((CELLS, C), BF), dma((16,))],
        compiler_params=pltpu.CompilerParams(vmem_limit_bytes=58 * 2**20),
    )(grad_features, g_two, g_one)
    shape = (3, 3, C, HALF)
    return grad_features.reshape(features.shape), one.reshape(shape), two.reshape(shape)


def solution(mesh):
    placed = (
        P(("dp", "fsdp"), "spatial", None, None),
        P(("dp", "fsdp"), "spatial", None),
        P(("dp", "fsdp")),
        P(),
        P(),
        P(None, None, None, "fsdp"),
        P(None, None, None, "fsdp"),
        P(("dp", "fsdp"), "spatial", None, None),
    )
    return jax.shard_map(
        on_device,
        mesh=mesh,
        in_specs=placed,
        out_specs=(
            P(("dp", "fsdp"), "spatial", None, None),
            P(None, None, None, "fsdp"),
            P(None, None, None, "fsdp"),
        ),
        check_vma=False,
    )
```
